128 devices in a mesh: section: 4 (over z), expert: 4 (over x), tensor: 8 (over y, core).
Axes of the slice: x: 4, y: 4, z: 4, core: 2. Of those that a mesh axis runs over, the one named last changes fastest.
Arguments:
- update: bfloat16 [8, 7168, 2048], P('section', 'tensor', 'expert'), may hold values from -4 to 4
- residual: float32 [8, 7168, 2048], P('section', 'tensor', 'expert'), may hold values from -2 to 2
- kept_blocks: int32 [8, 8, 8, 4], P('section', 'tensor', 'expert'), may hold values from 0 to 13, as said below
- kept_count: int32 [8], replicated, may hold values from 2 to 4, as said below
- serving_slot: int32 [8], replicated, may hold values from 0 to 7, as said below
- served_up: bfloat16 [4, 8, 7168, 2048], P('section', 'expert', None, 'tensor'), may hold values from -6 to 6
Outputs:
- served_new: bfloat16 [4, 8, 7168, 2048], P('section', 'expert', None, 'tensor')
- residual_new: float32 [8, 7168, 2048], P('section', 'tensor', 'expert')
The draws below stay inside these ranges and needn't reach their ends.
Inputs may be any that keep to these rules, and one draw needn't show every extreme that they name: `kept_blocks`: the 4 entries of one row differ; each names one of the group's 14 blocks in row-major order: block row within the row range times (2) plus block column within the group's 256 hidden units. Expert e uses the first kept_count[e] slots of each of its rows of kept_blocks; some expert uses all 4. A permutation: expert e is served at position serving_slot[e], on device serving_slot[e] // 2 of the expert axis; experts trained on one section (equal e // 2) are served on different devices.
All inputs are finite; a program needn't handle non-finite values.
Results may differ from the reference program's by a relative error of at most 0.0039.
Values may be sent and summed in bfloat16 or wider, within the bound.
A program may use at most 128 MiB of HBM per device.

```python
import jax
import jax.numpy as jnp
from jax import lax

D = 7168
F = 2048
BLK = 128
EXP_DEV = 2
KEEP = 4
E = 8
E_SEC = 2
GW = 256
GROUPS = 8
NBI = 14
N_SECTION = 4
N_EXPERT = 4
N_TENSOR = 8


def draw_kept_blocks(key, part):
    key = jax.random.fold_in(key, 11)
    row_count = E * N_TENSOR * GROUPS
    scores = jax.random.randint(key, (row_count, NBI), 0, 1 << 20) * NBI + jnp.arange(NBI, dtype=jnp.int32)[None, :]
    ranked = jnp.argsort(scores, axis=1, stable=True)[:, :KEEP]
    return ranked.reshape(E, N_TENSOR, GROUPS, KEEP).astype(jnp.int32)


def draw_kept_count(key, part):
    key = jax.random.fold_in(key, 12)
    first_key, second_key = jax.random.split(key)
    levels = jax.random.randint(first_key, (E,), max(1, KEEP // 2), KEEP + 1)
    picked = jax.random.randint(second_key, (), 0, E)
    return jnp.where(jnp.arange(E, dtype=jnp.int32) == picked, KEEP, levels).astype(jnp.int32)


def draw_serving_slot(key, part):
    key = jax.random.fold_in(key, 13)
    first_key, second_key = jax.random.split(key)
    device_order = jax.random.permutation(first_key, N_EXPERT).astype(jnp.int32)
    scores = jax.random.randint(second_key, (N_EXPERT, EXP_DEV), 0, 1 << 20) * EXP_DEV + jnp.arange(EXP_DEV, dtype=jnp.int32)[None, :]
    slot_order = jnp.argsort(scores, axis=1, stable=True).astype(jnp.int32)
    experts_all = jnp.arange(E, dtype=jnp.int32)
    section_of = experts_all // E_SEC
    local_index = experts_all % E_SEC
    device_of = device_order[(section_of + local_index) % N_EXPERT]
    return (device_of * EXP_DEV + slot_order[device_of, local_index]).astype(jnp.int32)


def level_of(stream_key, shape, shards, smallest, top_value):
    gain, own = 1.0, jax.random.fold_in(stream_key, 6)
    for dim, blocks in shards:
        draws = jnp.exp(jax.random.uniform(jax.random.fold_in(own, dim), (blocks,), jnp.float32, smallest / len(shards), top_value / len(shards)))
        gain = gain * jnp.repeat(draws, shape[dim] // blocks).reshape([-1 if axis == dim else 1 for axis in range(len(shape))])
    return gain


def gaussian(own_key, shape, width, reach, cuts=(), held_as=jnp.bfloat16):
    loudness = level_of(own_key, shape, cuts, -0.22, 0.18) if cuts else 1.0
    result = jax.random.normal(own_key, shape, jnp.float32) * width * loudness
    return jnp.minimum(jnp.maximum(result, -reach), reach).astype(held_as)


def setup_inputs(seed: int = 0) -> dict:
    key_list = jax.random.split(jax.random.key(seed), 7)
    update = gaussian(key_list[0], (E, D, F), 0.5, 4.0, ((0, 4), (1, 8), (2, 4)))
    residual = gaussian(key_list[1], (E, D, F), 0.25, 2.0, ((0, 4), (1, 8), (2, 4)), jnp.float32)
    kept_blocks = draw_kept_blocks(jax.random.fold_in(key_list[6], 71), 0)
    kept_count = draw_kept_count(jax.random.fold_in(key_list[6], 71), 0)
    serving_slot = draw_serving_slot(jax.random.fold_in(key_list[6], 71), 0)
    served_up = gaussian(key_list[5], (N_SECTION, E, D, F), 1.0, 6.0, ((0, 4), (1, 4), (3, 8)))
    return {"update": update, "residual": residual, "kept_blocks": kept_blocks, "kept_count": kept_count, "serving_slot": serving_slot, "served_up": served_up}


def reference(update, residual, kept_blocks, kept_count, serving_slot, served_up):
    change = update.astype(jnp.float32) + residual
    group_blocks = GW // BLK
    rows_tensor = D // N_TENSOR // BLK
    keep_slots = jnp.arange(KEEP, dtype=jnp.int32)
    in_use = keep_slots[None, None, None, :] < kept_count[:, None, None, None]
    block_row = jnp.arange(N_TENSOR, dtype=jnp.int32)[None, :, None, None] * rows_tensor + kept_blocks // group_blocks
    block_col = jnp.arange(GROUPS, dtype=jnp.int32)[None, None, :, None] * group_blocks + kept_blocks % group_blocks
    expert_ids = jnp.broadcast_to(jnp.arange(E, dtype=jnp.int32)[:, None, None, None], kept_blocks.shape)
    covered = jnp.zeros((E, D // BLK, F // BLK), jnp.int32).at[expert_ids, block_row, block_col].add(in_use.astype(jnp.int32))
    covered = covered > 0
    rounded = change.astype(jnp.bfloat16)
    shaped = change.reshape(E, D // BLK, BLK, F // BLK, BLK)
    sent = jnp.where(covered[:, :, None, :, None], rounded.reshape(shaped.shape), jnp.zeros((), jnp.bfloat16))
    residual_new = (shaped - sent.astype(jnp.float32)).reshape(E, D, F)
    by_position = jnp.zeros((E, D, F), jnp.bfloat16).at[serving_slot].set(sent.reshape(E, D, F))

    def apply_copy(copy):
        return (copy.astype(jnp.float32) + by_position.astype(jnp.float32)).astype(jnp.bfloat16)

    served_new = lax.map(apply_copy, served_up)
    return served_new, residual_new
```

```python
import functools

import jax
import jax.numpy as jnp
from jax import lax
from jax.experimental import pallas as pl
from jax.experimental.pallas import tpu as pltpu
from jax.sharding import PartitionSpec as P

MESH = pl.DeviceIdType.MESH
BLK = 128
SECTIONS = 4
EXPERTS = 4
TENSORS = 8
OWN = 2
GROUPS = 2
KEEP = 4
ROW_BLOCKS = 7
WINDOW = 8
SLOTS_A = 2
CHUNKS_A = 4
CHUNKS_B = 4
ROWS_A = BLK // CHUNKS_A
SHARE_B = (KEEP - SLOTS_A) * BLK // SECTIONS
ROWS_B = SHARE_B // CHUNKS_B


def own_place():
    return lax.axis_index("section"), lax.axis_index("expert"), lax.axis_index("tensor")


def share_place(section, chunk):
    first = section * SHARE_B + chunk * ROWS_B
    return SLOTS_A + first // BLK, first % BLK


def pack_kernel(update, residual, kept, packed, numbers, upd, res, upd_sem, res_sem):
    picks = [(le, gl, j) for le in range(OWN) for gl in range(GROUPS) for j in range(KEEP)]
    copies = []
    for i, (le, gl, j) in enumerate(picks):
        code = kept[le, 0, gl, j]
        row = pl.multiple_of((code // 2) * BLK, BLK)
        column = pl.multiple_of((gl * 2 + code % 2) * BLK, BLK)
        at = (le, pl.ds(row, BLK), pl.ds(column, BLK))
        copies.append(
            (
                pltpu.make_async_copy(update.at[at], upd.at[i], upd_sem.at[i]),
                pltpu.make_async_copy(residual.at[at], res.at[i], res_sem.at[i]),
            )
        )
        for copy in copies[-1]:
            copy.start()
    lanes = lax.broadcasted_iota(jnp.int32, (1, BLK), 1)
    row = jnp.zeros((1, BLK), jnp.int32)
    for i, (le, gl, j) in enumerate(picks):
        row = jnp.where(lanes == i, kept[le, 0, gl, j], row)
    numbers[...] = row
    for i, (le, gl, j) in enumerate(picks):
        for copy in copies[i]:
            copy.wait()
        packed[le, gl, j] = (upd[i].astype(jnp.float32) + res[i]).astype(jnp.bfloat16)


def pack(update, residual, kept):
    n = OWN * GROUPS * KEEP
    hbm, vmem = pltpu.HBM, pltpu.VMEM
    return pl.pallas_call(
        pack_kernel,
        out_shape=(
            vmem((OWN, GROUPS, KEEP, BLK, BLK), jnp.bfloat16),
            vmem((1, BLK), jnp.int32),
        ),
        in_specs=[pl.BlockSpec(memory_space=m) for m in (hbm, hbm, pltpu.SMEM)],
        out_specs=(pl.BlockSpec(memory_space=vmem),) * 2,
        scratch_shapes=[
            vmem((n, BLK, BLK), jnp.bfloat16),
            vmem((n, BLK, BLK), jnp.float32),
            pltpu.SemaphoreType.DMA((n,)),
            pltpu.SemaphoreType.DMA((n,)),
        ],
        compiler_params=pltpu.CompilerParams(vmem_limit_bytes=16 << 20),
        name="pack",
    )(update, residual, kept)


def push_kernel(
    packed, numbers, update, residual, kept, count, slots, served,
    res_out, staged, fin_a, fin_b, fin_c,
    upd, sel, z_a, s_a, x_a, z_b, s_b, x_b, z_c, x_c,
    load_sem,
    a1_s, a1_r, a2_s, a2_r, a3_s, a3_r,
    b1_s, b1_r, b2_s, b2_r, b3_s, b3_r, b4_s, b4_r,
    c1_s, c1_r, c2_s, c2_r, c3_s, c3_r,
):
    z, x, t = own_place()
    up, down = (z + 1) % SECTIONS, (z + 3) % SECTIONS

    loads = []
    for le in range(OWN):
        loads.append(pltpu.make_async_copy(update.at[le], upd.at[le], load_sem.at[2 * le]))
        loads.append(pltpu.make_async_copy(residual.at[le], res_out.at[le], load_sem.at[2 * le + 1]))
    for load in loads:
        load.start()
    stage = pltpu.make_async_copy(served.at[0], staged, load_sem.at[4])
    stage.start()

    for p in range(WINDOW):
        for e in range(WINDOW):
            here = (slots[e] == p).astype(jnp.float32)
            sel[p, e] = jnp.full(sel.shape[2:], here, jnp.float32).astype(sel.dtype)
    z_c[z] = numbers[...]

    barrier = pltpu.get_barrier_semaphore()
    for d in range(1, SECTIONS):
        pl.semaphore_signal(barrier, inc=1, device_id=((z + d) % SECTIONS, x, t), device_id_type=MESH)
    for d in range(1, EXPERTS):
        pl.semaphore_signal(barrier, inc=1, device_id=(z, (x + d) % EXPERTS, t), device_id_type=MESH)
    for d in range(1, TENSORS):
        pl.semaphore_signal(barrier, inc=1, device_id=(z, x, (t + d) % TENSORS), device_id_type=MESH)

    pl.semaphore_wait(barrier, SECTIONS + EXPERTS + TENSORS - 3)

    def remote(src, dst, send, recv, to):
        return pltpu.make_async_remote_copy(
            src_ref=src, dst_ref=dst, send_sem=send, recv_sem=recv, device_id=to, device_id_type=MESH
        )

    def b1(q, d):
        to = (z + d) % SECTIONS
        slot, row = share_place(to, q)
        row = pl.multiple_of(row, ROWS_B)
        return remote(
            packed.at[:, :, slot, pl.ds(row, ROWS_B)], z_b.at[q, z], b1_s.at[q, d], b1_r.at[q, d], (to, x, t)
        )

    def ring(buffer, send, recv, q, half, leap, going_up):
        own = (z + SECTIONS - leap) % SECTIONS if going_up else (z + leap) % SECTIONS
        n = buffer.shape[2] // 2
        ref = buffer.at[q, own, pl.ds(half * n, n)]
        i = 2 * (0 if going_up else 1) + half if leap == 0 else 4 + half
        return remote(ref, ref, send.at[q, i], recv.at[q, i], (up if going_up else down, x, t))

    def a1(q, half, leap, going_up):
        return ring(z_a, a1_s, a1_r, q, half, leap, going_up)

    def b4(q, half, leap, going_up):
        return ring(fin_b, b4_s, b4_r, q, half, leap, going_up)

    def hop_x(sorted_, got, send, recv, q, d):
        return remote(
            sorted_.at[q, d], got.at[q, x], send.at[q, d], recv.at[q, d], (z, (x + d) % EXPERTS, t)
        )

    def hop_y(got, fin, send, recv, q, source, gl):
        return remote(
            got.at[q, source, gl], fin, send.at[q, source * 2 + gl], recv.at[q, t], (z, x, source * 2 + gl)
        )

    def ring_start(copy, q):
        copy(q, 0, 0, True).start()
        copy(q, 1, 0, False).start()
        copy(q, 1, 0, True).start()
        copy(q, 0, 0, False).start()

    def ring_forward(copy, q):
        copy(q, 0, 0, True).wait_recv()
        copy(q, 0, 1, True).start()
        copy(q, 1, 0, False).wait_recv()
        copy(q, 1, 1, False).start()

    def ring_finish(copy, q):
        copy(q, 1, 0, True).wait_recv()
        copy(q, 0, 0, False).wait_recv()
        copy(q, 0, 1, True).wait_recv()
        copy(q, 1, 1, False).wait_recv()

    def ring_sent(copy, q):
        for half in range(2):
            copy(q, half, 0, True).wait_send()
            copy(q, half, 0, False).wait_send()
        copy(q, 0, 1, True).wait_send()
        copy(q, 1, 1, False).wait_send()

    def sort(gathered, sorted_, got, q):
        for d in range(EXPERTS):
            to = (x + d) % EXPERTS
            for place in range(OWN):
                p = to * OWN + place
                picks = [sel[p, e] for e in range(WINDOW)]
                for gl in range(GROUPS):
                    shape = gathered.shape[4:]
                    value = None
                    for e in range(WINDOW):
                        part = gathered[q, e // OWN, e % OWN, gl].reshape(-1, 16, BLK) * picks[e][None]
                        value = part if value is None else value + part
                    value = value.reshape(shape)
                    if d == 0:
                        got[q, x, gl, place] = value
                    else:
                        sorted_[q, d, gl, place] = value

    def start_y(got, fin_of, send, recv, q, source):
        for gl in range(GROUPS):
            here = source * 2 + gl == t

            @pl.when(jnp.logical_not(here))
            def _():
                hop_y(got, fin_of(q, t), send, recv, q, source, gl).start()

            @pl.when(here)
            def _():
                fin_of(q, t)[...] = got[q, source, gl]

    def sent_y(got, fin_of, send, recv, q):
        for d in range(1, TENSORS):
            to = (t + d) % TENSORS
            hop_y(got, fin_of(q, t), send, recv, q, to // 2, to % 2).wait_send()

    def got_y(got, fin_of, send, recv, q):
        for d in range(1, TENSORS):
            source = (t + d) % TENSORS
            ref = fin_of(q, source)
            remote(ref, ref, send.at[q, source], recv.at[q, source], (z, x, source)).wait_recv()

    def route(gathered, sorted_, got, fin_of, x_s, x_r, y_s, y_r, q):
        sort(gathered, sorted_, got, q)
        for d in range(1, EXPERTS):
            hop_x(sorted_, got, x_s, x_r, q, d).start()
        start_y(got, fin_of, y_s, y_r, q, x)

    def pass_on(sorted_, got, fin_of, x_s, x_r, y_s, y_r, q):
        for d in range(1, EXPERTS):
            hop_x(sorted_, got, x_s, x_r, q, d).wait_recv()
            start_y(got, fin_of, y_s, y_r, q, (x + EXPERTS - d) % EXPERTS)

    def fin_a_of(q, source):
        return fin_a.at[q, source]

    def fin_b_of(q, source):
        return fin_b.at[q, z, source]

    def c1(d):
        return remote(z_c.at[z], z_c.at[z], c1_s.at[d], c1_r.at[d], ((z + d) % SECTIONS, x, t))

    def c2(d):
        return remote(z_c, x_c.at[x], c2_s.at[d], c2_r.at[d], (z, (x + d) % EXPERTS, t))

    def c3(source, gl):
        to = source * 2 + gl
        return remote(x_c.at[source], fin_c.at[t], c3_s.at[to], c3_r.at[t], (z, x, to))

    def got_c3(source):
        ref = fin_c.at[source]
        return remote(ref, ref, c3_s.at[source], c3_r.at[source], (z, x, source))

    def numbers_along_x():
        for d in range(1, SECTIONS):
            c1(d).wait_recv()
        for d in range(1, EXPERTS):
            c2(d).start()
        x_c[x] = z_c[...]

    def numbers_along_y():
        for d in range(1, EXPERTS):
            c2(d).wait_recv()
        for d in range(1, TENSORS):
            to = (t + d) % TENSORS
            c3(to // 2, to % 2).start()
        fin_c[t] = x_c[t // 2]

    for d in range(1, SECTIONS):
        c1(d).start()

    def begin_b(q, _):
        for d in (2, 1, 3):
            b1(q, d).start()
        slot, row = share_place(z, q)
        row = pl.multiple_of(row, ROWS_B)
        for le in range(OWN):
            for gl in range(GROUPS):
                z_b[q, z, le, gl] = packed[le, gl, slot, pl.ds(row, ROWS_B)]
        return 0

    def begin_a(q, _):
        row = pl.multiple_of(q * ROWS_A, ROWS_A)
        for le in range(OWN):
            for gl in range(GROUPS):
                z_a[q, z, le, gl] = packed[le, gl, pl.ds(0, SLOTS_A), pl.ds(row, ROWS_A)]
        ring_start(a1, q)
        return 0

    lax.fori_loop(0, CHUNKS_B, begin_b, 0)
    if SLOTS_A:
        lax.fori_loop(0, CHUNKS_A, begin_a, 0)

    def keep_rest(i, _):
        le, r = i // ROW_BLOCKS, i % ROW_BLOCKS
        row = pl.multiple_of(r * BLK, BLK)
        limit = count[z * OWN + le]
        for column in range(2 * GROUPS):
            block = r * 2 + column % 2
            sent = 0
            for j in range(KEEP):
                chosen = (kept[le, 0, column // 2, j] == block).astype(jnp.int32)
                sent = sent + chosen * (j < limit).astype(jnp.int32)
            sent = sent.astype(jnp.float32)
            at = (le, pl.ds(row, BLK), pl.ds(column * BLK, BLK))
            change = upd[at].astype(jnp.float32) + res_out[at]
            rounded = change.astype(jnp.bfloat16).astype(jnp.float32)
            res_out[at] = change - sent * rounded
        return 0

    for load in loads:
        load.wait()
    lax.fori_loop(0, OWN * ROW_BLOCKS, keep_rest, 0)
    numbers_along_x()

    route_b = functools.partial(route, z_b, s_b, x_b, fin_b_of, b2_s, b2_r, b3_s, b3_r)
    pass_b = functools.partial(pass_on, s_b, x_b, fin_b_of, b2_s, b2_r, b3_s, b3_r)
    route_a = functools.partial(route, z_a, s_a, x_a, fin_a_of, a2_s, a2_r, a3_s, a3_r)
    pass_a = functools.partial(pass_on, s_a, x_a, fin_a_of, a2_s, a2_r, a3_s, a3_r)

    def b_p1(q):
        for d in range(1, SECTIONS):
            b1(q, d).wait_recv()
        route_b(q)

    def b_p3(q):
        got_y(x_b, fin_b_of, b3_s, b3_r, q)
        ring_start(b4, q)

    def a_p2(q):
        ring_finish(a1, q)
        route_a(q)

    steps = [
        (CHUNKS_B, 0, b_p1),
        (CHUNKS_A if SLOTS_A else 0, 0, lambda q: ring_forward(a1, q)),
        (CHUNKS_B, 1, pass_b),
        (CHUNKS_B, 2, b_p3),
        (CHUNKS_A if SLOTS_A else 0, 1, a_p2),
        (CHUNKS_A if SLOTS_A else 0, 2, pass_a),
        (CHUNKS_B, 4, lambda q: ring_forward(b4, q)),
    ]

    def step(s, _):
        pl.when(s == 1)(numbers_along_y)
        for n, lag, work in steps:
            if n:
                pl.when((s >= lag) & (s < lag + n))(functools.partial(work, s - lag))
        return 0

    lax.fori_loop(0, max(n + lag for n, lag, _ in steps if n), step, 0)

    def end_b(q, _):
        ring_finish(b4, q)
        for d in range(1, SECTIONS):
            b1(q, d).wait_send()
        for d in range(1, EXPERTS):
            hop_x(s_b, x_b, b2_s, b2_r, q, d).wait_send()
        sent_y(x_b, fin_b_of, b3_s, b3_r, q)
        ring_sent(b4, q)
        return 0

    def end_a(q, _):
        got_y(x_a, fin_a_of, a3_s, a3_r, q)
        ring_sent(a1, q)
        for d in range(1, EXPERTS):
            hop_x(s_a, x_a, a2_s, a2_r, q, d).wait_send()
        sent_y(x_a, fin_a_of, a3_s, a3_r, q)
        return 0

    if SLOTS_A:
        lax.fori_loop(0, CHUNKS_A, end_a, 0)
    lax.fori_loop(0, CHUNKS_B, end_b, 0)
    for d in range(1, SECTIONS):
        c1(d).wait_send()
    for d in range(1, EXPERTS):
        c2(d).wait_send()
    for d in range(1, TENSORS):
        to = (t + d) % TENSORS
        got_c3(to).wait_recv()
        c3(to // 2, to % 2).wait_send()
    stage.wait()


def push(packed, numbers, update, residual, kept, count, slots, served):
    bf = jnp.bfloat16
    hbm, smem, vmem = pltpu.HBM, pltpu.SMEM, pltpu.VMEM
    ca, cb = CHUNKS_A, CHUNKS_B
    sa = max(SLOTS_A, 1)
    sems = []
    for chunks, width in ((ca, 6), (ca, 4), (ca, 8), (cb, 4), (cb, 4), (cb, 8), (cb, 6)):
        sems += [pltpu.SemaphoreType.DMA((chunks, width))] * 2
    for width in (4, 4, 8):
        sems += [pltpu.SemaphoreType.DMA((width,))] * 2
    return pl.pallas_call(
        push_kernel,
        out_shape=(
            vmem(residual.shape, jnp.float32),
            vmem(served.shape[1:], bf),
            vmem((ca, TENSORS, OWN, sa, ROWS_A, BLK), bf),
            vmem((cb, SECTIONS, TENSORS, OWN, ROWS_B, BLK), bf),
            vmem((TENSORS, SECTIONS, 1, BLK), jnp.int32),
        ),
        in_specs=[
            pl.BlockSpec(memory_space=vmem),
            pl.BlockSpec(memory_space=vmem),
            pl.BlockSpec(memory_space=hbm),
            pl.BlockSpec(memory_space=hbm),
            pl.BlockSpec(memory_space=smem),
            pl.BlockSpec(memory_space=smem),
            pl.BlockSpec(memory_space=smem),
            pl.BlockSpec(memory_space=hbm),
        ],
        out_specs=(pl.BlockSpec(memory_space=vmem),) * 5,
        scratch_shapes=[
            vmem(update.shape, bf),
            vmem((WINDOW, WINDOW, 16, BLK), bf),
            vmem((ca, SECTIONS, OWN, GROUPS, sa, ROWS_A, BLK), bf),
            vmem((ca, EXPERTS, GROUPS, OWN, sa, ROWS_A, BLK), bf),
            vmem((ca, EXPERTS, GROUPS, OWN, sa, ROWS_A, BLK), bf),
            vmem((cb, SECTIONS, OWN, GROUPS, ROWS_B, BLK), bf),
            vmem((cb, EXPERTS, GROUPS, OWN, ROWS_B, BLK), bf),
            vmem((cb, EXPERTS, GROUPS, OWN, ROWS_B, BLK), bf),
            vmem((SECTIONS, 1, BLK), jnp.int32),
            vmem((EXPERTS, SECTIONS, 1, BLK), jnp.int32),
            pltpu.SemaphoreType.DMA((5,)),
            *sems,
        ],
        compiler_params=pltpu.CompilerParams(
            collective_id=0, has_side_effects=True, vmem_limit_bytes=48 << 20
        ),
        name="push",
    )(packed, numbers, update, residual, kept, count, slots, served)


def apply_kernel(codes, count, slots, staged_in, fin_a, fin_b, out, staged, sem):
    del staged_in
    _, x, t = own_place()

    def region(place, source):
        rows = ROW_BLOCKS * BLK
        at = pl.ds(pl.multiple_of(source * rows, rows), rows)
        return pltpu.make_async_copy(staged.at[place, at], out.at[0, place, at], sem)

    for place in range(OWN):
        p = x * OWN + place
        e = sum(jnp.where(slots[i] == p, i, 0) for i in range(WINDOW))
        limit = count[e]
        base = (e % OWN) * GROUPS * KEEP + (t % GROUPS) * KEEP

        def row_range(source, _):
            for j in range(KEEP):
                code = codes[source, e // OWN, 0, base + j]

                @pl.when(j < limit)
                def _():
                    row = source * (ROW_BLOCKS * BLK) + (code // 2) * BLK
                    column = pl.ds(pl.multiple_of((code % 2) * BLK, BLK), BLK)

                    def add(first, rows, piece):
                        at = (place, pl.ds(pl.multiple_of(row + first, 16), rows), column)
                        total = staged[at].astype(jnp.float32) + piece.astype(jnp.float32)
                        staged[at] = total.astype(jnp.bfloat16)

                    if j < SLOTS_A:
                        for q in range(CHUNKS_A):
                            add(q * ROWS_A, ROWS_A, fin_a[q, source, place, j])
                    else:
                        for section in range(SECTIONS):
                            for q in range(CHUNKS_B):
                                slot, first = share_place(section, q)
                                if slot == j:
                                    add(first, ROWS_B, fin_b[q, section, source, place])

            region(place, source).start()
            return 0

        lax.fori_loop(0, TENSORS, row_range, 0)

    for place in range(OWN):
        for source in range(TENSORS):
            region(place, source).wait()


def apply(codes, count, slots, staged, fin_a, fin_b, served):
    smem, vmem = pltpu.SMEM, pltpu.VMEM
    return pl.pallas_call(
        apply_kernel,
        out_shape=(
            jax.ShapeDtypeStruct(served.shape, served.dtype),
            vmem(staged.shape, staged.dtype),
        ),
        in_specs=[pl.BlockSpec(memory_space=smem)] * 3 + [pl.BlockSpec(memory_space=vmem)] * 3,
        out_specs=(pl.BlockSpec(memory_space=pltpu.HBM), pl.BlockSpec(memory_space=vmem)),
        scratch_shapes=[pltpu.SemaphoreType.DMA],
        input_output_aliases={3: 1},
        compiler_params=pltpu.CompilerParams(vmem_limit_bytes=32 << 20),
        name="apply",
    )(codes, count, slots, staged, fin_a, fin_b)[0]


def on_device(update, residual, kept_blocks, kept_count, serving_slot, served_up):
    packed, numbers = pack(update, residual, kept_blocks)
    res_new, staged, fin_a, fin_b, codes = push(
        packed, numbers, update, residual, kept_blocks, kept_count, serving_slot, served_up
    )
    served_new = apply(codes, kept_count, serving_slot, staged, fin_a, fin_b, served_up)
    return served_new, res_new


def solution(mesh):
    return jax.shard_map(
        on_device,
        mesh=mesh,
        in_specs=(
            P("section", "tensor", "expert"),
            P("section", "tensor", "expert"),
            P("section", "tensor", "expert", None),
            P(),
            P(),
            P("section", "expert", None, "tensor"),
        ),
        out_specs=(P("section", "expert", None, "tensor"), P("section", "tensor", "expert")),
        check_vma=False,
    )
```

```python
import functools

import jax
import jax.numpy as jnp
from jax import lax
from jax.experimental import pallas as pl
from jax.experimental.pallas import tpu as pltpu
from jax.sharding import PartitionSpec as P

MESH = pl.DeviceIdType.MESH
BLK = 128
SECTIONS = 4
EXPERTS = 4
TENSORS = 8
OWN = 2
GROUPS = 2
KEEP = 4
ROW_BLOCKS = 7
WINDOW = 8
SLOTS_A = 1
CHUNKS_A = 2
CHUNKS_B = 6
ROWS_A = BLK // CHUNKS_A
SHARE_B = (KEEP - SLOTS_A) * BLK // SECTIONS
ROWS_B = SHARE_B // CHUNKS_B


SCHEDULE = (
    "c", "b0", "b1", "b2", "b3", "b4", "b5", "a0", "a1", "l", "br0", "br1",
    "cr", "br2", "br3", "br4", "br5", "k", "af0", "bs0", "af1", "bs1", "ar0", "bs2",
    "bf0", "bs3", "ar1", "bs4", "bf1", "bf2", "bs5", "be0", "bf3", "bf4", "be1", "be2",
    "ae0", "bf5", "be3", "be4", "be5", "ae1", "ce",
)


def own_place():
    return lax.axis_index("section"), lax.axis_index("expert"), lax.axis_index("tensor")


def share_place(section, chunk):
    first = section * SHARE_B + chunk * ROWS_B
    return SLOTS_A + first // BLK, first % BLK


def push_kernel(
    update, residual, kept, count, slots, served,
    res_out, staged, fin_a, fin_b, fin_c,
    upd_0, upd_1, rest_0, rest_1, packed, sel, z_a, s_a, z_b, s_b, z_c,
    load_sem, stage_sem, a_send, a_up, a_down, a_far, a_got, b_send, b_in, b_got, b_up, b_down, b_far,
    c_send, c_in, c_got,
):
    z, x, t = own_place()
    up, down = ((z + 1) % SECTIONS, x, t), ((z + 3) % SECTIONS, x, t)
    on_diagonal = t // GROUPS == x

    upd, rest = (upd_0, upd_1), (rest_0, rest_1)
    loads = [[] for _ in range(OWN)]
    for le in range(OWN):
        for column in range(2 * GROUPS):
            lanes = pl.ds(column * BLK, BLK)
            for n, (src, dst) in enumerate(((update, upd[le]), (residual, rest[le]))):
                dst = dst.at[column // 2, pl.ds(column % 2 * ROW_BLOCKS, ROW_BLOCKS)]
                loads[le].append(
                    pltpu.make_async_copy(src.at[le, :, :, lanes], dst, load_sem.at[le, 2 * column + n])
                )
    stage = pltpu.make_async_copy(served.at[0], staged, stage_sem)
    for load in (*loads[0], *loads[1]):
        load.start()

    barrier = pltpu.get_barrier_semaphore()
    for d in range(1, SECTIONS):
        pl.semaphore_signal(barrier, inc=1, device_id=((z + d) % SECTIONS, x, t), device_id_type=MESH)
    for d in range(TENSORS):
        to = (t + d) % TENSORS

        def greet(to=to):
            pl.semaphore_signal(barrier, inc=1, device_id=(z, t // GROUPS, to), device_id_type=MESH)

        if d == 0:
            pl.when(jnp.logical_not(on_diagonal))(greet)
        else:
            greet()

    for p in range(WINDOW):
        for e in range(WINDOW):
            here = (slots[e] == p).astype(jnp.float32)
            sel[p, e] = jnp.full(sel.shape[2:], here, jnp.float32).astype(sel.dtype)
    lanes = lax.broadcasted_iota(jnp.int32, (1, BLK), 1)
    numbers = jnp.zeros((1, BLK), jnp.int32)
    for i in range(OWN * GROUPS * KEEP):
        number = kept[i // (GROUPS * KEEP), 0, i // KEEP % GROUPS, i % KEEP]
        numbers = numbers + number * (lanes == i).astype(jnp.int32)
    z_c[z] = numbers

    for le in range(OWN):
        for load in loads[le]:
            load.wait()
        for gl in range(GROUPS):
            for j in range(KEEP):
                number = kept[le, 0, gl, j]
                at = (gl, (number & 1) * ROW_BLOCKS + (number >> 1))
                change = upd[le][at].astype(jnp.float32) + rest[le][at]
                packed[le, gl, j] = change.astype(jnp.bfloat16)
    pl.semaphore_wait(barrier, SECTIONS - 1 + TENSORS - on_diagonal.astype(jnp.int32))

    def remote(src, dst, send, recv, to):
        return pltpu.make_async_remote_copy(
            src_ref=src, dst_ref=dst, send_sem=send, recv_sem=recv, device_id=to, device_id_type=MESH
        )

    def wait_for(ref, sem):
        pltpu.make_async_copy(ref, ref, sem).wait()

    def across(src_of, dst, send, got):
        for d in range(EXPERTS):
            for gl in range(GROUPS):
                to = x * GROUPS + gl
                src = src_of(d, gl)
                copy = remote(src, dst, send, got, (z, (x + d) % EXPERTS, to))
                if d:
                    copy.start()
                else:
                    own = pltpu.make_async_copy(src, dst, got)
                    pl.when(to != t)(copy.start)
                    pl.when(to == t)(own.start)

    def across_sent(whole, send):
        n = whole.shape[0]

        @pl.when(on_diagonal)
        def _():
            wait_for(whole.at[pl.ds(0, n - n // TENSORS)], send)

        @pl.when(jnp.logical_not(on_diagonal))
        def _():
            wait_for(whole, send)

    def sort(gathered, sorted_, q):
        for d in range(EXPERTS):
            for place in range(OWN):
                p = (x + d) % EXPERTS * OWN + place
                picks = [sel[p, e] for e in range(WINDOW)]
                for gl in range(GROUPS):
                    value = None
                    for e in range(WINDOW):
                        part = gathered[q, e // OWN, e % OWN, gl].reshape(-1, 16, BLK) * picks[e][None]
                        value = part if value is None else value + part
                    sorted_[q, d, gl, place] = value.reshape(gathered.shape[4:])

    def ring_start(buffer, q, send, go_up, go_down):
        ref = buffer.at[q, z]
        remote(ref, ref, send, go_up.at[q], up).start()
        remote(ref, ref, send, go_down.at[q], down).start()

    def ring_forward(buffer, q, send, go_up, go_down, far):
        if q % 2 == 0:
            ref = buffer.at[q, (z + 3) % SECTIONS]
            wait_for(ref, go_up.at[q])
            remote(ref, ref, send, far.at[q], up).start()
        else:
            ref = buffer.at[q, (z + 1) % SECTIONS]
            wait_for(ref, go_down.at[q])
            remote(ref, ref, send, far.at[q], down).start()

    def ring_finish(buffer, q, go_up, go_down, far):
        ref = buffer.at[q, z]
        wait_for(ref, (go_down if q % 2 == 0 else go_up).at[q])
        wait_for(ref, far.at[q])

    def share_of(section, q):
        slot, row = share_place(section, q)
        return packed.at[:, :, slot, pl.ds(pl.multiple_of(row, ROWS_B), ROWS_B)]

    def b_begin(q):
        for d in (2, 1, 3):
            to = (z + d) % SECTIONS
            remote(share_of(to, q), z_b.at[q, z], b_send.at[0, q], b_in.at[q], (to, x, t)).start()
        z_b[q, z] = share_of(z, q)[...]

    def b_route(q):
        wait_for(z_b.at[q, pl.ds(0, SECTIONS - 1)], b_in.at[q])
        sort(z_b, s_b, q)
        across(lambda d, gl: s_b.at[q, d, gl], fin_b.at[q, z, t], b_send.at[1, q], b_got.at[q])

    def b_spread(q):
        wait_for(fin_b.at[q, z], b_got.at[q])
        ring_start(fin_b, q, b_send.at[2, q], b_up, b_down)

    def b_forward(q):
        ring_forward(fin_b, q, b_send.at[2, q], b_up, b_down, b_far)

    def b_finish(q):
        ring_finish(fin_b, q, b_up, b_down, b_far)

    def a_begin(q):
        z_a[q, z] = packed[:, :, pl.ds(0, SLOTS_A), pl.ds(q * ROWS_A, ROWS_A)]
        ring_start(z_a, q, a_send.at[0, q], a_up, a_down)

    def a_forward(q):
        ring_forward(z_a, q, a_send.at[0, q], a_up, a_down, a_far)

    def a_route(q):
        ring_finish(z_a, q, a_up, a_down, a_far)
        sort(z_a, s_a, q)
        across(lambda d, gl: s_a.at[q, d, gl], fin_a.at[q, t], a_send.at[1, q], a_got.at[q])

    def a_finish(q):
        wait_for(fin_a.at[q], a_got.at[q])

    def c_begin(_):
        for d in range(1, SECTIONS):
            remote(z_c.at[z], z_c.at[z], c_send.at[0], c_in, ((z + d) % SECTIONS, x, t)).start()

    def c_route(_):
        wait_for(z_c.at[pl.ds(0, SECTIONS - 1)], c_in)
        across(lambda d, gl: z_c, fin_c.at[t], c_send.at[1], c_got)

    def c_finish(_):
        wait_for(fin_c, c_got)

    def load_served(_):
        stage.start()

    def keep_rest(_):
        for le in range(OWN):
            limit = count[z * OWN + le]

            def row_block(r, _, le=le, limit=limit):
                row = pl.ds(pl.multiple_of(r * BLK, BLK), BLK)
                for column in range(2 * GROUPS):
                    block = r * 2 + column % 2
                    sent = 0
                    for j in range(KEEP):
                        chosen = (kept[le, 0, column // 2, j] == block).astype(jnp.int32)
                        sent = sent + chosen * (j < limit).astype(jnp.int32)
                    sent = sent.astype(jnp.float32)
                    at = (column // 2, column % 2 * ROW_BLOCKS + r)
                    change = upd[le][at].astype(jnp.float32) + rest[le][at]
                    rounded = change.astype(jnp.bfloat16).astype(jnp.float32)
                    res_out[le, row, pl.ds(column * BLK, BLK)] = change - sent * rounded
                return 0

            lax.fori_loop(0, ROW_BLOCKS, row_block, 0)

    work = {
        "b": b_begin, "br": b_route, "bs": b_spread, "bf": b_forward, "be": b_finish,
        "a": a_begin, "af": a_forward, "ar": a_route, "ae": a_finish,
        "c": c_begin, "cr": c_route, "ce": c_finish, "k": keep_rest, "l": load_served,
    }
    for item in SCHEDULE:
        name = item.rstrip("0123456789")
        work[name](int(item[len(name) :] or 0))

    for q in range(CHUNKS_B):
        wait_for(z_b.at[q, pl.ds(0, SECTIONS - 1)], b_send.at[0, q])
        across_sent(fin_b.at[q, z], b_send.at[1, q])
        wait_for(fin_b.at[q, pl.ds(0, 3)], b_send.at[2, q])
    for q in range(CHUNKS_A):
        wait_for(z_a.at[q, pl.ds(0, 3)], a_send.at[0, q])
        across_sent(fin_a.at[q], a_send.at[1, q])
    wait_for(z_c.at[pl.ds(0, SECTIONS - 1)], c_send.at[0])
    across_sent(fin_c, c_send.at[1])
    stage.wait()


def by_rows(array):
    return array.reshape(OWN, ROW_BLOCKS, BLK, array.shape[-1])


def push(update, residual, kept, count, slots, served):
    bf = jnp.bfloat16
    hbm, smem, vmem = pltpu.HBM, pltpu.SMEM, pltpu.VMEM
    ca, cb = CHUNKS_A, CHUNKS_B
    dma = pltpu.SemaphoreType.DMA
    return pl.pallas_call(
        push_kernel,
        out_shape=(
            vmem(residual.shape, jnp.float32),
            vmem(served.shape[1:], bf),
            vmem((ca, TENSORS, OWN, SLOTS_A, ROWS_A, BLK), bf),
            vmem((cb, SECTIONS, TENSORS, OWN, ROWS_B, BLK), bf),
            vmem((TENSORS, SECTIONS, 1, BLK), jnp.int32),
        ),
        in_specs=[pl.BlockSpec(memory_space=m) for m in (hbm, hbm, smem, smem, smem, hbm)],
        out_specs=(pl.BlockSpec(memory_space=vmem),) * 5,
        scratch_shapes=[
            *[vmem((GROUPS, 2 * ROW_BLOCKS, BLK, BLK), bf)] * OWN,
            *[vmem((GROUPS, 2 * ROW_BLOCKS, BLK, BLK), jnp.float32)] * OWN,
            vmem((OWN, GROUPS, KEEP, BLK, BLK), bf),
            vmem((WINDOW, WINDOW, 16, BLK), bf),
            vmem((ca, SECTIONS, OWN, GROUPS, SLOTS_A, ROWS_A, BLK), bf),
            vmem((ca, EXPERTS, GROUPS, OWN, SLOTS_A, ROWS_A, BLK), bf),
            vmem((cb, SECTIONS, OWN, GROUPS, ROWS_B, BLK), bf),
            vmem((cb, EXPERTS, GROUPS, OWN, ROWS_B, BLK), bf),
            vmem((SECTIONS, 1, BLK), jnp.int32),
            dma((OWN, 4 * GROUPS)),
            dma,
            *[dma((2, ca)), dma((ca,)), dma((ca,)), dma((ca,)), dma((ca,))],
            *[dma((3, cb)), dma((cb,)), dma((cb,)), dma((cb,)), dma((cb,)), dma((cb,))],
            *[dma((2,)), dma, dma],
        ],
        compiler_params=pltpu.CompilerParams(
            collective_id=0, has_side_effects=True, vmem_limit_bytes=45 << 20
        ),
        name="push",
    )(by_rows(update), by_rows(residual), kept, count, slots, served)


def apply_kernel(codes, count, slots, rest, staged_in, fin_a, fin_b, out, rest_out, staged, sem, rest_sem):
    del staged_in
    rest_copy = pltpu.make_async_copy(rest, rest_out, rest_sem)
    rest_copy.start()
    _, x, t = own_place()

    def region(place, source):
        rows = ROW_BLOCKS * BLK
        at = pl.ds(pl.multiple_of(source * rows, rows), rows)
        return pltpu.make_async_copy(staged.at[place, at], out.at[0, place, at], sem)

    for place in range(OWN):
        p = x * OWN + place
        e = sum(jnp.where(slots[i] == p, i, 0) for i in range(WINDOW))
        limit = count[e]
        base = (e % OWN) * GROUPS * KEEP + (t % GROUPS) * KEEP

        def row_range(source, _):
            for j in range(KEEP):
                code = codes[source, e // OWN, 0, base + j]

                @pl.when(j < limit)
                def _():
                    row = source * (ROW_BLOCKS * BLK) + (code // 2) * BLK
                    column = pl.ds(pl.multiple_of((code % 2) * BLK, BLK), BLK)

                    def add(first, rows, piece):
                        at = (place, pl.ds(pl.multiple_of(row + first, 16), rows), column)
                        total = staged[at].astype(jnp.float32) + piece.astype(jnp.float32)
                        staged[at] = total.astype(jnp.bfloat16)

                    if j < SLOTS_A:
                        for q in range(CHUNKS_A):
                            add(q * ROWS_A, ROWS_A, fin_a[q, source, place, j])
                    else:
                        for section in range(SECTIONS):
                            for q in range(CHUNKS_B):
                                slot, first = share_place(section, q)
                                if slot == j:
                                    add(first, ROWS_B, fin_b[q, section, source, place])

            region(place, source).start()
            return 0

        lax.fori_loop(0, TENSORS, row_range, 0)

    for place in range(OWN):
        for source in range(TENSORS):
            region(place, source).wait()
    rest_copy.wait()


def apply(codes, count, slots, rest, staged, fin_a, fin_b, served):
    smem, vmem = pltpu.SMEM, pltpu.VMEM
    return pl.pallas_call(
        apply_kernel,
        out_shape=(
            jax.ShapeDtypeStruct(served.shape, served.dtype),
            jax.ShapeDtypeStruct(rest.shape, rest.dtype),
            vmem(staged.shape, staged.dtype),
        ),
        in_specs=[pl.BlockSpec(memory_space=smem)] * 3 + [pl.BlockSpec(memory_space=vmem)] * 4,
        out_specs=[pl.BlockSpec(memory_space=m) for m in (pltpu.HBM, pltpu.HBM, vmem)],
        scratch_shapes=[pltpu.SemaphoreType.DMA] * 2,
        input_output_aliases={4: 2},
        compiler_params=pltpu.CompilerParams(vmem_limit_bytes=32 << 20),
        name="apply",
    )(codes, count, slots, rest, staged, fin_a, fin_b)[:2]


def on_device(update, residual, kept_blocks, kept_count, serving_slot, served_up):
    res_new, staged, fin_a, fin_b, codes = push(
        update, residual, kept_blocks, kept_count, serving_slot, served_up
    )
    return apply(codes, kept_count, serving_slot, res_new, staged, fin_a, fin_b, served_up)


def solution(mesh):
    return jax.shard_map(
        on_device,
        mesh=mesh,
        in_specs=(
            P("section", "tensor", "expert"),
            P("section", "tensor", "expert"),
            P("section", "tensor", "expert", None),
            P(),
            P(),
            P("section", "expert", None, "tensor"),
        ),
        out_specs=(P("section", "expert", None, "tensor"), P("section", "tensor", "expert")),
        check_vma=False,
    )
```

```python
import functools

import jax
import jax.numpy as jnp
from jax import lax
from jax.experimental import pallas as pl
from jax.experimental.pallas import tpu as pltpu
from jax.sharding import PartitionSpec as P

MESH = pl.DeviceIdType.MESH
BLK = 128
SECTIONS = 4
EXPERTS = 4
TENSORS = 8
OWN = 2
GROUPS = 2
KEEP = 4
ROW_BLOCKS = 7
WINDOW = 8
SLOTS_A = 1
CHUNKS_A = 2
CHUNKS_B = 6
ROWS_A = BLK // CHUNKS_A
SHARE_B = (KEEP - SLOTS_A) * BLK // SECTIONS
ROWS_B = SHARE_B // CHUNKS_B


DIRECT_B = (5,)

SCHEDULE = (
    "c", "b0", "b1", "b2", "b3", "b4", "b5", "a0", "a1", "l", "br0", "br1",
    "br2", "br3", "br4", "br5", "cr", "k", "af0", "bs0", "af1", "bs1", "ar0", "bs2",
    "bf0", "bs3", "ar1", "bs4", "bf1", "bs5", "bf2", "be0", "bf3", "bf4", "be1", "be2",
    "ae0", "be3", "be4", "be5", "ae1", "ce",
)


def own_place():
    return lax.axis_index("section"), lax.axis_index("expert"), lax.axis_index("tensor")


def share_place(section, chunk):
    first = section * SHARE_B + chunk * ROWS_B
    return SLOTS_A + first // BLK, first % BLK


def push_kernel(
    update, residual, kept, count, slots, served,
    res_out, staged, fin_a, fin_b, fin_c,
    upd_0, upd_1, rest_0, rest_1, packed, sel, z_a, s_a, z_b, s_b, z_c,
    load_sem, stage_sem, a_send, a_up, a_down, a_far, a_got, b_send, b_in, b_got, b_up, b_down, b_far,
    c_send, c_in, c_got,
):
    z, x, t = own_place()
    up, down = ((z + 1) % SECTIONS, x, t), ((z + 3) % SECTIONS, x, t)
    on_diagonal = t // GROUPS == x

    barrier = pltpu.get_barrier_semaphore()
    for d in range(1, SECTIONS):
        pl.semaphore_signal(barrier, inc=1, device_id=((z + d) % SECTIONS, x, t), device_id_type=MESH)
    for d in range(TENSORS):
        to = (t + d) % TENSORS

        def greet(to=to):
            pl.semaphore_signal(barrier, inc=1, device_id=(z, t // GROUPS, to), device_id_type=MESH)

        if d == 0:
            pl.when(jnp.logical_not(on_diagonal))(greet)
        else:
            greet()

    upd, rest = (upd_0, upd_1), (rest_0, rest_1)
    loads = [[] for _ in range(OWN)]
    for le in range(OWN):
        for column in range(2 * GROUPS):
            lanes = pl.ds(column * BLK, BLK)
            for n, (src, dst) in enumerate(((update, upd[le]), (residual, rest[le]))):
                dst = dst.at[column // 2, pl.ds(column % 2 * ROW_BLOCKS, ROW_BLOCKS)]
                loads[le].append(
                    pltpu.make_async_copy(src.at[le, :, :, lanes], dst, load_sem.at[le, 2 * column + n])
                )
    stage = pltpu.make_async_copy(served.at[0], staged, stage_sem)
    for load in (*loads[0], *loads[1]):
        load.start()

    for p in range(WINDOW):
        for e in range(WINDOW):
            here = (slots[e] == p).astype(jnp.float32)
            sel[p, e] = jnp.full(sel.shape[2:], here, jnp.float32).astype(sel.dtype)
    lanes = lax.broadcasted_iota(jnp.int32, (1, BLK), 1)
    numbers = jnp.zeros((1, BLK), jnp.int32)
    for i in range(OWN * GROUPS * KEEP):
        number = kept[i // (GROUPS * KEEP), 0, i // KEEP % GROUPS, i % KEEP]
        numbers = numbers + number * (lanes == i).astype(jnp.int32)
    z_c[z] = numbers

    for le in range(OWN):
        for load in loads[le]:
            load.wait()
        for gl in range(GROUPS):
            for j in range(KEEP):
                number = kept[le, 0, gl, j]
                at = (gl, (number & 1) * ROW_BLOCKS + (number >> 1))
                change = upd[le][at].astype(jnp.float32) + rest[le][at]
                packed[le, gl, j] = change.astype(jnp.bfloat16)
    pl.semaphore_wait(barrier, SECTIONS - 1 + TENSORS - on_diagonal.astype(jnp.int32))

    def remote(src, dst, send, recv, to):
        return pltpu.make_async_remote_copy(
            src_ref=src, dst_ref=dst, send_sem=send, recv_sem=recv, device_id=to, device_id_type=MESH
        )

    def wait_for(ref, sem):
        pltpu.make_async_copy(ref, ref, sem).wait()

    def across(src_of, dst, send, got):
        for d in range(EXPERTS):
            for gl in range(GROUPS):
                to = x * GROUPS + gl
                src = src_of(d, gl)
                copy = remote(src, dst, send, got, (z, (x + d) % EXPERTS, to))
                if d:
                    copy.start()
                else:
                    own = pltpu.make_async_copy(src, dst, got)
                    pl.when(to != t)(copy.start)
                    pl.when(to == t)(own.start)

    def across_sent(whole, send):
        n = whole.shape[0]

        @pl.when(on_diagonal)
        def _():
            wait_for(whole.at[pl.ds(0, n - n // TENSORS)], send)

        @pl.when(jnp.logical_not(on_diagonal))
        def _():
            wait_for(whole, send)

    def sort(gathered, sorted_, q):
        for d in range(EXPERTS):
            for place in range(OWN):
                p = (x + d) % EXPERTS * OWN + place
                picks = [sel[p, e] for e in range(WINDOW)]
                for gl in range(GROUPS):
                    value = None
                    for e in range(WINDOW):
                        part = gathered[q, e // OWN, e % OWN, gl].reshape(-1, 16, BLK) * picks[e][None]
                        value = part if value is None else value + part
                    sorted_[q, d, gl, place] = value.reshape(gathered.shape[4:])

    def ring_start(buffer, q, send, go_up, go_down, far=None):
        ref = buffer.at[q, z]
        remote(ref, ref, send, go_up.at[q], up).start()
        remote(ref, ref, send, go_down.at[q], down).start()
        if far is not None:
            remote(ref, ref, send, far.at[q], ((z + 2) % SECTIONS, x, t)).start()

    def ring_forward(buffer, q, send, go_up, go_down, far):
        n = buffer.shape[2] // 2
        for half, source, got, to in ((0, (z + 3) % SECTIONS, go_up, up), (1, (z + 1) % SECTIONS, go_down, down)):
            wait_for(buffer.at[q, source], got.at[q])
            ref = buffer.at[q, source, pl.ds(half * n, n)]
            remote(ref, ref, send, far.at[q], to).start()

    def ring_finish(buffer, q, go_up, go_down, far, direct=False):
        ref = buffer.at[q, z]
        if direct:
            wait_for(ref, go_up.at[q])
            wait_for(ref, go_down.at[q])
        wait_for(ref, far.at[q])

    def share_of(section, q):
        slot, row = share_place(section, q)
        return packed.at[:, :, slot, pl.ds(pl.multiple_of(row, ROWS_B), ROWS_B)]

    def b_begin(q):
        for d in (2, 1, 3):
            to = (z + d) % SECTIONS
            remote(share_of(to, q), z_b.at[q, z], b_send.at[0, q], b_in.at[q], (to, x, t)).start()
        z_b[q, z] = share_of(z, q)[...]

    def b_route(q):
        wait_for(z_b.at[q, pl.ds(0, SECTIONS - 1)], b_in.at[q])
        sort(z_b, s_b, q)
        across(lambda d, gl: s_b.at[q, d, gl], fin_b.at[q, z, t], b_send.at[1, q], b_got.at[q])

    def b_spread(q):
        wait_for(fin_b.at[q, z], b_got.at[q])
        ring_start(fin_b, q, b_send.at[2, q], b_up, b_down, b_far if q in DIRECT_B else None)

    def b_forward(q):
        ring_forward(fin_b, q, b_send.at[2, q], b_up, b_down, b_far)

    def b_finish(q):
        ring_finish(fin_b, q, b_up, b_down, b_far, q in DIRECT_B)

    def a_begin(q):
        z_a[q, z] = packed[:, :, pl.ds(0, SLOTS_A), pl.ds(q * ROWS_A, ROWS_A)]
        ring_start(z_a, q, a_send.at[0, q], a_up, a_down)

    def a_forward(q):
        ring_forward(z_a, q, a_send.at[0, q], a_up, a_down, a_far)

    def a_route(q):
        ring_finish(z_a, q, a_up, a_down, a_far)
        sort(z_a, s_a, q)
        across(lambda d, gl: s_a.at[q, d, gl], fin_a.at[q, t], a_send.at[1, q], a_got.at[q])

    def a_finish(q):
        wait_for(fin_a.at[q], a_got.at[q])

    def c_begin(_):
        for d in range(1, SECTIONS):
            remote(z_c.at[z], z_c.at[z], c_send.at[0], c_in, ((z + d) % SECTIONS, x, t)).start()

    def c_route(_):
        wait_for(z_c.at[pl.ds(0, SECTIONS - 1)], c_in)
        across(lambda d, gl: z_c, fin_c.at[t], c_send.at[1], c_got)

    def c_finish(_):
        wait_for(fin_c, c_got)

    def load_served(_):
        stage.start()

    def keep_rest(_):
        for le in range(OWN):
            limit = count[z * OWN + le]

            def row_block(r, _, le=le, limit=limit):
                row = pl.ds(pl.multiple_of(r * BLK, BLK), BLK)
                for column in range(2 * GROUPS):
                    block = r * 2 + column % 2
                    sent = 0
                    for j in range(KEEP):
                        chosen = (kept[le, 0, column // 2, j] == block).astype(jnp.int32)
                        sent = sent + chosen * (j < limit).astype(jnp.int32)
                    sent = sent.astype(jnp.float32)
                    at = (column // 2, column % 2 * ROW_BLOCKS + r)
                    change = upd[le][at].astype(jnp.float32) + rest[le][at]
                    rounded = change.astype(jnp.bfloat16).astype(jnp.float32)
                    res_out[le, row, pl.ds(column * BLK, BLK)] = change - sent * rounded
                return 0

            lax.fori_loop(0, ROW_BLOCKS, row_block, 0)

    work = {
        "b": b_begin, "br": b_route, "bs": b_spread, "bf": b_forward, "be": b_finish,
        "a": a_begin, "af": a_forward, "ar": a_route, "ae": a_finish,
        "c": c_begin, "cr": c_route, "ce": c_finish, "k": keep_rest, "l": load_served,
    }
    for item in SCHEDULE:
        name = item.rstrip("0123456789")
        work[name](int(item[len(name) :] or 0))

    for q in range(CHUNKS_B):
        wait_for(z_b.at[q, pl.ds(0, SECTIONS - 1)], b_send.at[0, q])
        across_sent(fin_b.at[q, z], b_send.at[1, q])
        wait_for(fin_b.at[q, pl.ds(0, 3)], b_send.at[2, q])
    for q in range(CHUNKS_A):
        wait_for(z_a.at[q, pl.ds(0, 3)], a_send.at[0, q])
        across_sent(fin_a.at[q], a_send.at[1, q])
    wait_for(z_c.at[pl.ds(0, SECTIONS - 1)], c_send.at[0])
    across_sent(fin_c, c_send.at[1])
    stage.wait()


def by_rows(array):
    return array.reshape(OWN, ROW_BLOCKS, BLK, array.shape[-1])


def push(update, residual, kept, count, slots, served):
    bf = jnp.bfloat16
    hbm, smem, vmem = pltpu.HBM, pltpu.SMEM, pltpu.VMEM
    ca, cb = CHUNKS_A, CHUNKS_B
    dma = pltpu.SemaphoreType.DMA
    return pl.pallas_call(
        push_kernel,
        out_shape=(
            vmem(residual.shape, jnp.float32),
            vmem(served.shape[1:], bf),
            vmem((ca, TENSORS, OWN, SLOTS_A, ROWS_A, BLK), bf),
            vmem((cb, SECTIONS, TENSORS, OWN, ROWS_B, BLK), bf),
            vmem((TENSORS, SECTIONS, 1, BLK), jnp.int32),
        ),
        in_specs=[pl.BlockSpec(memory_space=m) for m in (hbm, hbm, smem, smem, smem, hbm)],
        out_specs=(pl.BlockSpec(memory_space=vmem),) * 5,
        scratch_shapes=[
            *[vmem((GROUPS, 2 * ROW_BLOCKS, BLK, BLK), bf)] * OWN,
            *[vmem((GROUPS, 2 * ROW_BLOCKS, BLK, BLK), jnp.float32)] * OWN,
            vmem((OWN, GROUPS, KEEP, BLK, BLK), bf),
            vmem((WINDOW, WINDOW, 16, BLK), bf),
            vmem((ca, SECTIONS, OWN, GROUPS, SLOTS_A, ROWS_A, BLK), bf),
            vmem((ca, EXPERTS, GROUPS, OWN, SLOTS_A, ROWS_A, BLK), bf),
            vmem((cb, SECTIONS, OWN, GROUPS, ROWS_B, BLK), bf),
            vmem((cb, EXPERTS, GROUPS, OWN, ROWS_B, BLK), bf),
            vmem((SECTIONS, 1, BLK), jnp.int32),
            dma((OWN, 4 * GROUPS)),
            dma,
            *[dma((2, ca)), dma((ca,)), dma((ca,)), dma((ca,)), dma((ca,))],
            *[dma((3, cb)), dma((cb,)), dma((cb,)), dma((cb,)), dma((cb,)), dma((cb,))],
            *[dma((2,)), dma, dma],
        ],
        compiler_params=pltpu.CompilerParams(
            collective_id=0, has_side_effects=True, vmem_limit_bytes=45 << 20
        ),
        name="push",
    )(by_rows(update), by_rows(residual), kept, count, slots, served)


def apply_kernel(codes, count, slots, rest, staged_in, fin_a, fin_b, out, rest_out, staged, sem, rest_sem):
    del staged_in
    rest_copy = pltpu.make_async_copy(rest, rest_out, rest_sem)
    rest_copy.start()
    _, x, t = own_place()

    def region(place, source):
        rows = ROW_BLOCKS * BLK
        at = pl.ds(pl.multiple_of(source * rows, rows), rows)
        return pltpu.make_async_copy(staged.at[place, at], out.at[0, place, at], sem)

    for place in range(OWN):
        p = x * OWN + place
        e = sum(jnp.where(slots[i] == p, i, 0) for i in range(WINDOW))
        limit = count[e]
        base = (e % OWN) * GROUPS * KEEP + (t % GROUPS) * KEEP

        def row_range(source, _):
            for j in range(KEEP):
                code = codes[source, e // OWN, 0, base + j]

                @pl.when(j < limit)
                def _():
                    row = source * (ROW_BLOCKS * BLK) + (code // 2) * BLK
                    column = pl.ds(pl.multiple_of((code % 2) * BLK, BLK), BLK)

                    def add(first, rows, piece):
                        at = (place, pl.ds(pl.multiple_of(row + first, 16), rows), column)
                        total = staged[at].astype(jnp.float32) + piece.astype(jnp.float32)
                        staged[at] = total.astype(jnp.bfloat16)

                    if j < SLOTS_A:
                        for q in range(CHUNKS_A):
                            add(q * ROWS_A, ROWS_A, fin_a[q, source, place, j])
                    else:
                        for section in range(SECTIONS):
                            for q in range(CHUNKS_B):
                                slot, first = share_place(section, q)
                                if slot == j:
                                    add(first, ROWS_B, fin_b[q, section, source, place])

            region(place, source).start()
            return 0

        lax.fori_loop(0, TENSORS, row_range, 0)

    for place in range(OWN):
        for source in range(TENSORS):
            region(place, source).wait()
    rest_copy.wait()


def apply(codes, count, slots, rest, staged, fin_a, fin_b, served):
    smem, vmem = pltpu.SMEM, pltpu.VMEM
    return pl.pallas_call(
        apply_kernel,
        out_shape=(
            jax.ShapeDtypeStruct(served.shape, served.dtype),
            jax.ShapeDtypeStruct(rest.shape, rest.dtype),
            vmem(staged.shape, staged.dtype),
        ),
        in_specs=[pl.BlockSpec(memory_space=smem)] * 3 + [pl.BlockSpec(memory_space=vmem)] * 4,
        out_specs=[pl.BlockSpec(memory_space=m) for m in (pltpu.HBM, pltpu.HBM, vmem)],
        scratch_shapes=[pltpu.SemaphoreType.DMA] * 2,
        input_output_aliases={4: 2},
        compiler_params=pltpu.CompilerParams(vmem_limit_bytes=32 << 20),
        name="apply",
    )(codes, count, slots, rest, staged, fin_a, fin_b)[:2]


def on_device(update, residual, kept_blocks, kept_count, serving_slot, served_up):
    res_new, staged, fin_a, fin_b, codes = push(
        update, residual, kept_blocks, kept_count, serving_slot, served_up
    )
    return apply(codes, kept_count, serving_slot, res_new, staged, fin_a, fin_b, served_up)


def solution(mesh):
    return jax.shard_map(
        on_device,
        mesh=mesh,
        in_specs=(
            P("section", "tensor", "expert"),
            P("section", "tensor", "expert"),
            P("section", "tensor", "expert", None),
            P(),
            P(),
            P("section", "expert", None, "tensor"),
        ),
        out_specs=(P("section", "expert", None, "tensor"), P("section", "tensor", "expert")),
        check_vma=False,
    )
```

```python
import functools

import jax
import jax.numpy as jnp
from jax import lax
from jax.experimental import pallas as pl
from jax.experimental.pallas import tpu as pltpu
from jax.sharding import PartitionSpec as P

MESH = pl.DeviceIdType.MESH
BLK = 128
SECTIONS = 4
EXPERTS = 4
TENSORS = 8
OWN = 2
GROUPS = 2
KEEP = 4
ROW_BLOCKS = 7
WINDOW = 8
SLOTS_A = 1
CHUNKS_A = 1
CHUNKS_B = 3
ROWS_A = BLK // CHUNKS_A
SHARE_B = (KEEP - SLOTS_A) * BLK // SECTIONS
ROWS_B = SHARE_B // CHUNKS_B


SCHEDULE = (
    "c", "b0", "b3", "b1", "b4", "b2", "b5", "a0", "a1", "l", "br0", "br3",
    "br1", "br4", "br2", "br5", "cr", "k", "af0", "bs0", "bs3", "af1", "bs1", "bs4",
    "ar0", "bs2", "bs5", "bf0", "bf3", "ar1", "bf1", "bf4", "bf2", "bf5", "be0", "be3",
    "be1", "be4", "be2", "be5", "ae0", "ae1", "ce",
)


def own_place():
    return lax.axis_index("section"), lax.axis_index("expert"), lax.axis_index("tensor")


def share_place(section, chunk):
    first = section * SHARE_B + chunk * ROWS_B
    return SLOTS_A + first // BLK, first % BLK


def push_kernel(
    update, residual, kept, count, slots, served,
    res_out, staged, fin_a, fin_b, fin_c,
    upd_0, upd_1, rest_0, rest_1, packed, sel, z_a, s_a, z_b, s_b, z_c,
    load_sem, stage_sem, a_send, a_up, a_down, a_far, a_got, b_send, b_ring, b_in, b_got, b_up, b_down, b_far,
    c_send, c_in, c_got,
):
    z, x, t = own_place()
    up, down = ((z + 1) % SECTIONS, x, t), ((z + 3) % SECTIONS, x, t)
    on_diagonal = t // GROUPS == x

    barrier = pltpu.get_barrier_semaphore()
    for d in range(1, SECTIONS):
        pl.semaphore_signal(barrier, inc=1, device_id=((z + d) % SECTIONS, x, t), device_id_type=MESH)
    for d in range(TENSORS):
        to = (t + d) % TENSORS

        def greet(to=to):
            pl.semaphore_signal(barrier, inc=1, device_id=(z, t // GROUPS, to), device_id_type=MESH)

        if d == 0:
            pl.when(jnp.logical_not(on_diagonal))(greet)
        else:
            greet()

    upd, rest = (upd_0, upd_1), (rest_0, rest_1)
    loads = [[] for _ in range(OWN)]
    for le in range(OWN):
        for column in range(2 * GROUPS):
            lanes = pl.ds(column * BLK, BLK)
            for n, (src, dst) in enumerate(((update, upd[le]), (residual, rest[le]))):
                dst = dst.at[column // 2, pl.ds(column % 2 * ROW_BLOCKS, ROW_BLOCKS)]
                loads[le].append(
                    pltpu.make_async_copy(src.at[le, :, :, lanes], dst, load_sem.at[le, 2 * column + n])
                )
    stage = pltpu.make_async_copy(served.at[0], staged, stage_sem)
    for load in (*loads[0], *loads[1]):
        load.start()

    for p in range(WINDOW):
        for e in range(WINDOW):
            here = (slots[e] == p).astype(jnp.float32)
            sel[p, e] = jnp.full(sel.shape[2:], here, jnp.float32).astype(sel.dtype)
    lanes = lax.broadcasted_iota(jnp.int32, (1, BLK), 1)
    numbers = jnp.zeros((1, BLK), jnp.int32)
    for i in range(OWN * GROUPS * KEEP):
        number = kept[i // (GROUPS * KEEP), 0, i // KEEP % GROUPS, i % KEEP]
        numbers = numbers + number * (lanes == i).astype(jnp.int32)
    z_c[z] = numbers

    for le in range(OWN):
        for load in loads[le]:
            load.wait()
        for gl in range(GROUPS):
            for j in range(KEEP):
                number = kept[le, 0, gl, j]
                at = (gl, (number & 1) * ROW_BLOCKS + (number >> 1))
                change = upd[le][at].astype(jnp.float32) + rest[le][at]
                packed[le, gl, j] = change.astype(jnp.bfloat16)
    pl.semaphore_wait(barrier, SECTIONS - 1 + TENSORS - on_diagonal.astype(jnp.int32))

    def remote(src, dst, send, recv, to):
        return pltpu.make_async_remote_copy(
            src_ref=src, dst_ref=dst, send_sem=send, recv_sem=recv, device_id=to, device_id_type=MESH
        )

    def wait_for(ref, sem):
        pltpu.make_async_copy(ref, ref, sem).wait()

    def across(src_of, dst, send, got, gl):
        to = x * GROUPS + gl
        for d in range(EXPERTS):
            src = src_of(d)
            copy = remote(src, dst, send, got, (z, (x + d) % EXPERTS, to))
            if d:
                copy.start()
            else:
                own = pltpu.make_async_copy(src, dst, got)
                pl.when(to != t)(copy.start)
                pl.when(to == t)(own.start)

    def across_sent(whole, send, gl):
        to = x * GROUPS + gl

        @pl.when(to == t)
        def _():
            wait_for(whole.at[pl.ds(0, EXPERTS - 1)], send)

        @pl.when(to != t)
        def _():
            wait_for(whole.at[pl.ds(0, EXPERTS)], send)

    def on_core(gl):
        return pl.when(t % GROUPS == gl)

    def sort(gathered, sorted_, q):
        for d in range(EXPERTS):
            for place in range(OWN):
                p = (x + d) % EXPERTS * OWN + place
                value = None
                for e in range(WINDOW):
                    part = gathered[q, e // OWN, e % OWN].reshape(-1, 16, BLK) * sel[p, e][None]
                    value = part if value is None else value + part
                sorted_[q, d, place] = value.reshape(gathered.shape[3:])

    def ring_start(buffer, q, send, go_up, go_down):
        ref = buffer.at[q, z]
        remote(ref, ref, send, go_up.at[q], up).start()
        remote(ref, ref, send, go_down.at[q], down).start()

    def ring_forward(buffer, q, send, go_up, go_down, far):
        n = buffer.shape[2] // 2
        for half, source, got, to in ((0, (z + 3) % SECTIONS, go_up, up), (1, (z + 1) % SECTIONS, go_down, down)):
            wait_for(buffer.at[q, source], got.at[q])
            ref = buffer.at[q, source, pl.ds(half * n, n)]
            remote(ref, ref, send, far.at[q], to).start()

    def ring_finish(buffer, q, far):
        wait_for(buffer.at[q, z], far.at[q])

    def share_of(section, q):
        slot, row = share_place(section, q % CHUNKS_B)
        return packed.at[:, q // CHUNKS_B, slot, pl.ds(pl.multiple_of(row, ROWS_B), ROWS_B)]

    def b_begin(q):
        for d in (2, 1, 3):
            to = (z + d) % SECTIONS
            remote(share_of(to, q), z_b.at[q, z], b_send.at[0, q], b_in.at[q], (to, x, t)).start()
        z_b[q, z] = share_of(z, q)[...]

    def b_route(q):
        gl, i = q // CHUNKS_B, q % CHUNKS_B
        wait_for(z_b.at[q, pl.ds(0, SECTIONS - 1)], b_in.at[q])
        sort(z_b, s_b, q)
        across(lambda d: s_b.at[q, d], fin_b.at[i, z, t], b_send.at[1, q], b_got.at[i], gl)

    def b_spread(q):
        gl, i = q // CHUNKS_B, q % CHUNKS_B

        @on_core(gl)
        def _():
            wait_for(fin_b.at[i, z], b_got.at[i])
            ring_start(fin_b, i, b_ring.at[i], b_up, b_down)

    def b_forward(q):
        i = q % CHUNKS_B

        @on_core(q // CHUNKS_B)
        def _():
            ring_forward(fin_b, i, b_ring.at[i], b_up, b_down, b_far)

    def b_finish(q):
        i = q % CHUNKS_B

        @on_core(q // CHUNKS_B)
        def _():
            ring_finish(fin_b, i, b_far)

    def a_begin(q):
        rows = pl.ds(q % CHUNKS_A * ROWS_A, ROWS_A)
        z_a[q, z] = packed[:, q // CHUNKS_A, pl.ds(0, SLOTS_A), rows]
        ring_start(z_a, q, a_send.at[0, q], a_up, a_down)

    def a_forward(q):
        ring_forward(z_a, q, a_send.at[0, q], a_up, a_down, a_far)

    def a_route(q):
        gl, i = q // CHUNKS_A, q % CHUNKS_A
        ring_finish(z_a, q, a_far)
        sort(z_a, s_a, q)
        across(lambda d: s_a.at[q, d], fin_a.at[i, t], a_send.at[1, q], a_got.at[i], gl)

    def a_finish(q):
        i = q % CHUNKS_A

        @on_core(q // CHUNKS_A)
        def _():
            wait_for(fin_a.at[i], a_got.at[i])

    def c_begin(_):
        for d in range(1, SECTIONS):
            remote(z_c.at[z], z_c.at[z], c_send.at[0], c_in, ((z + d) % SECTIONS, x, t)).start()

    def c_route(_):
        wait_for(z_c.at[pl.ds(0, SECTIONS - 1)], c_in)
        for gl in range(GROUPS):
            across(lambda d: z_c, fin_c.at[t], c_send.at[1 + gl], c_got, gl)

    def c_finish(_):
        wait_for(fin_c, c_got)

    def load_served(_):
        stage.start()

    def keep_rest(_):
        for le in range(OWN):
            limit = count[z * OWN + le]

            def row_block(r, _, le=le, limit=limit):
                row = pl.ds(pl.multiple_of(r * BLK, BLK), BLK)
                for column in range(2 * GROUPS):
                    block = r * 2 + column % 2
                    sent = 0
                    for j in range(KEEP):
                        chosen = (kept[le, 0, column // 2, j] == block).astype(jnp.int32)
                        sent = sent + chosen * (j < limit).astype(jnp.int32)
                    sent = sent.astype(jnp.float32)
                    at = (column // 2, column % 2 * ROW_BLOCKS + r)
                    change = upd[le][at].astype(jnp.float32) + rest[le][at]
                    rounded = change.astype(jnp.bfloat16).astype(jnp.float32)
                    res_out[le, row, pl.ds(column * BLK, BLK)] = change - sent * rounded
                return 0

            lax.fori_loop(0, ROW_BLOCKS, row_block, 0)

    work = {
        "b": b_begin, "br": b_route, "bs": b_spread, "bf": b_forward, "be": b_finish,
        "a": a_begin, "af": a_forward, "ar": a_route, "ae": a_finish,
        "c": c_begin, "cr": c_route, "ce": c_finish, "k": keep_rest, "l": load_served,
    }
    for item in SCHEDULE:
        name = item.rstrip("0123456789")
        work[name](int(item[len(name) :] or 0))

    for q in range(GROUPS * CHUNKS_B):
        wait_for(z_b.at[q, pl.ds(0, SECTIONS - 1)], b_send.at[0, q])
        across_sent(s_b.at[q], b_send.at[1, q], q // CHUNKS_B)
    for i in range(CHUNKS_B):
        wait_for(fin_b.at[i, pl.ds(0, 3)], b_ring.at[i])
    for q in range(GROUPS * CHUNKS_A):
        wait_for(z_a.at[q, pl.ds(0, 3)], a_send.at[0, q])
        across_sent(s_a.at[q], a_send.at[1, q], q // CHUNKS_A)
    wait_for(z_c.at[pl.ds(0, SECTIONS - 1)], c_send.at[0])
    for gl in range(GROUPS):
        across_sent(fin_c, c_send.at[1 + gl], gl)
    stage.wait()


def by_rows(array):
    return array.reshape(OWN, ROW_BLOCKS, BLK, array.shape[-1])


def push(update, residual, kept, count, slots, served):
    bf = jnp.bfloat16
    hbm, smem, vmem = pltpu.HBM, pltpu.SMEM, pltpu.VMEM
    ca, cb = CHUNKS_A, CHUNKS_B
    na, nb = GROUPS * ca, GROUPS * cb
    dma = pltpu.SemaphoreType.DMA
    return pl.pallas_call(
        push_kernel,
        out_shape=(
            vmem(residual.shape, jnp.float32),
            vmem(served.shape[1:], bf),
            vmem((ca, TENSORS, OWN, SLOTS_A, ROWS_A, BLK), bf),
            vmem((cb, SECTIONS, TENSORS, OWN, ROWS_B, BLK), bf),
            vmem((TENSORS, SECTIONS, 1, BLK), jnp.int32),
        ),
        in_specs=[pl.BlockSpec(memory_space=m) for m in (hbm, hbm, smem, smem, smem, hbm)],
        out_specs=(pl.BlockSpec(memory_space=vmem),) * 5,
        scratch_shapes=[
            *[vmem((GROUPS, 2 * ROW_BLOCKS, BLK, BLK), bf)] * OWN,
            *[vmem((GROUPS, 2 * ROW_BLOCKS, BLK, BLK), jnp.float32)] * OWN,
            vmem((OWN, GROUPS, KEEP, BLK, BLK), bf),
            vmem((WINDOW, WINDOW, 16, BLK), bf),
            vmem((na, SECTIONS, OWN, SLOTS_A, ROWS_A, BLK), bf),
            vmem((na, EXPERTS, OWN, SLOTS_A, ROWS_A, BLK), bf),
            vmem((nb, SECTIONS, OWN, ROWS_B, BLK), bf),
            vmem((nb, EXPERTS, OWN, ROWS_B, BLK), bf),
            vmem((SECTIONS, 1, BLK), jnp.int32),
            dma((OWN, 4 * GROUPS)),
            dma,
            *[dma((2, na)), dma((na,)), dma((na,)), dma((na,)), dma((ca,))],
            *[dma((2, nb)), dma((cb,)), dma((nb,)), dma((cb,)), dma((cb,)), dma((cb,)), dma((cb,))],
            *[dma((3,)), dma, dma],
        ],
        compiler_params=pltpu.CompilerParams(
            collective_id=0, has_side_effects=True, vmem_limit_bytes=45 << 20
        ),
        name="push",
    )(by_rows(update), by_rows(residual), kept, count, slots, served)


def apply_kernel(codes, count, slots, rest, staged_in, fin_a, fin_b, out, rest_out, staged, sem, rest_sem):
    del staged_in
    rest_copy = pltpu.make_async_copy(rest, rest_out, rest_sem)
    rest_copy.start()
    _, x, t = own_place()

    def region(place, source):
        rows = ROW_BLOCKS * BLK
        at = pl.ds(pl.multiple_of(source * rows, rows), rows)
        return pltpu.make_async_copy(staged.at[place, at], out.at[0, place, at], sem)

    for place in range(OWN):
        p = x * OWN + place
        e = sum(jnp.where(slots[i] == p, i, 0) for i in range(WINDOW))
        limit = count[e]
        base = (e % OWN) * GROUPS * KEEP + (t % GROUPS) * KEEP

        def row_range(source, _):
            for j in range(KEEP):
                code = codes[source, e // OWN, 0, base + j]

                @pl.when(j < limit)
                def _():
                    row = source * (ROW_BLOCKS * BLK) + (code // 2) * BLK
                    column = pl.ds(pl.multiple_of((code % 2) * BLK, BLK), BLK)

                    def add(first, rows, piece):
                        at = (place, pl.ds(pl.multiple_of(row + first, 16), rows), column)
                        total = staged[at].astype(jnp.float32) + piece.astype(jnp.float32)
                        staged[at] = total.astype(jnp.bfloat16)

                    if j < SLOTS_A:
                        for q in range(CHUNKS_A):
                            add(q * ROWS_A, ROWS_A, fin_a[q, source, place, j])
                    else:
                        for section in range(SECTIONS):
                            for q in range(CHUNKS_B):
                                slot, first = share_place(section, q)
                                if slot == j:
                                    add(first, ROWS_B, fin_b[q, section, source, place])

            region(place, source).start()
            return 0

        lax.fori_loop(0, TENSORS, row_range, 0)

    for place in range(OWN):
        for source in range(TENSORS):
            region(place, source).wait()
    rest_copy.wait()


def apply(codes, count, slots, rest, staged, fin_a, fin_b, served):
    smem, vmem = pltpu.SMEM, pltpu.VMEM
    return pl.pallas_call(
        apply_kernel,
        out_shape=(
            jax.ShapeDtypeStruct(served.shape, served.dtype),
            jax.ShapeDtypeStruct(rest.shape, rest.dtype),
            vmem(staged.shape, staged.dtype),
        ),
        in_specs=[pl.BlockSpec(memory_space=smem)] * 3 + [pl.BlockSpec(memory_space=vmem)] * 4,
        out_specs=[pl.BlockSpec(memory_space=m) for m in (pltpu.HBM, pltpu.HBM, vmem)],
        scratch_shapes=[pltpu.SemaphoreType.DMA] * 2,
        input_output_aliases={4: 2},
        compiler_params=pltpu.CompilerParams(vmem_limit_bytes=32 << 20),
        name="apply",
    )(codes, count, slots, rest, staged, fin_a, fin_b)[:2]


def on_device(update, residual, kept_blocks, kept_count, serving_slot, served_up):
    res_new, staged, fin_a, fin_b, codes = push(
        update, residual, kept_blocks, kept_count, serving_slot, served_up
    )
    return apply(codes, kept_count, serving_slot, res_new, staged, fin_a, fin_b, served_up)


def solution(mesh):
    return jax.shard_map(
        on_device,
        mesh=mesh,
        in_specs=(
            P("section", "tensor", "expert"),
            P("section", "tensor", "expert"),
            P("section", "tensor", "expert", None),
            P(),
            P(),
            P("section", "expert", None, "tensor"),
        ),
        out_specs=(P("section", "expert", None, "tensor"), P("section", "tensor", "expert")),
        check_vma=False,
    )
```

```python
import functools

import jax
import jax.numpy as jnp
from jax import lax
from jax.experimental import pallas as pl
from jax.experimental.pallas import tpu as pltpu
from jax.sharding import PartitionSpec as P

MESH = pl.DeviceIdType.MESH
BLK = 128
SECTIONS = 4
EXPERTS = 4
TENSORS = 8
OWN = 2
GROUPS = 2
KEEP = 4
ROW_BLOCKS = 7
WINDOW = 8
SLOTS_A = 1
CHUNKS_A = 1
CHUNKS_B = 3
ROWS_A = BLK // CHUNKS_A
SHARE_B = (KEEP - SLOTS_A) * BLK // SECTIONS
ROWS_B = SHARE_B // CHUNKS_B


SCHEDULE = (
    "c", "b0", "b3", "b1", "b4", "b2", "b5", "a0", "a1", "l", "br0", "br3",
    "br1", "br4", "br2", "br5", "cr", "k", "af0", "bs0", "bs3", "af1", "bs1", "bs4",
    "ar0", "bs2", "bs5", "bf0", "bf3", "ar1", "bf1", "bf4", "bf2", "bf5", "be0", "be3",
    "be1", "be4", "be2", "be5", "ae0", "ae1", "ce",
)


def own_place():
    return lax.axis_index("section"), lax.axis_index("expert"), lax.axis_index("tensor")


def share_place(section, chunk):
    first = section * SHARE_B + chunk * ROWS_B
    return SLOTS_A + first // BLK, first % BLK


def push_kernel(
    update, residual, kept, count, slots, served,
    res_out, staged, fin_a, fin_b, fin_c,
    upd_0, upd_1, rest_0, rest_1, packed, sel, z_a, s_a, z_b, s_b, z_c,
    load_sem, stage_sem, a_send, a_up, a_down, a_far, a_got, b_send, b_ring, b_in, b_got, b_up, b_down, b_far,
    c_send, c_in, c_got,
):
    z, x, t = own_place()
    up, down = ((z + 1) % SECTIONS, x, t), ((z + 3) % SECTIONS, x, t)
    on_diagonal = t // GROUPS == x

    barrier = pltpu.get_barrier_semaphore()
    for d in range(1, SECTIONS):
        pl.semaphore_signal(barrier, inc=1, device_id=((z + d) % SECTIONS, x, t), device_id_type=MESH)
    for d in range(TENSORS):
        to = (t + d) % TENSORS

        def greet(to=to):
            pl.semaphore_signal(barrier, inc=1, device_id=(z, t // GROUPS, to), device_id_type=MESH)

        if d == 0:
            pl.when(jnp.logical_not(on_diagonal))(greet)
        else:
            greet()

    upd, rest = (upd_0, upd_1), (rest_0, rest_1)
    loads = [[] for _ in range(OWN)]
    for le in range(OWN):
        for column in range(2 * GROUPS):
            lanes = pl.ds(column * BLK, BLK)
            for n, (src, dst) in enumerate(((update, upd[le]), (residual, rest[le]))):
                dst = dst.at[column // 2, pl.ds(column % 2 * ROW_BLOCKS, ROW_BLOCKS)]
                loads[le].append(
                    pltpu.make_async_copy(src.at[le, :, :, lanes], dst, load_sem.at[le, 2 * column + n])
                )
    stage = pltpu.make_async_copy(served.at[0], staged, stage_sem)
    for load in (*loads[0], *loads[1]):
        load.start()

    for p in range(WINDOW):
        for e in range(WINDOW):
            here = (slots[e] == p).astype(jnp.float32)
            sel[p, e] = jnp.full(sel.shape[2:], here, jnp.float32).astype(sel.dtype)
    lanes = lax.broadcasted_iota(jnp.int32, (1, BLK), 1)
    numbers = jnp.zeros((1, BLK), jnp.int32)
    for i in range(OWN * GROUPS * KEEP):
        number = kept[i // (GROUPS * KEEP), 0, i // KEEP % GROUPS, i % KEEP]
        numbers = numbers + number * (lanes == i).astype(jnp.int32)
    z_c[z] = numbers

    for le in range(OWN):
        for load in loads[le]:
            load.wait()
        for gl in range(GROUPS):
            for j in range(KEEP):
                number = kept[le, 0, gl, j]
                at = (gl, (number & 1) * ROW_BLOCKS + (number >> 1))
                change = upd[le][at].astype(jnp.float32) + rest[le][at]
                packed[le, gl, j] = change.astype(jnp.bfloat16)
    pl.semaphore_wait(barrier, SECTIONS - 1 + TENSORS - on_diagonal.astype(jnp.int32))

    def remote(src, dst, send, recv, to):
        return pltpu.make_async_remote_copy(
            src_ref=src, dst_ref=dst, send_sem=send, recv_sem=recv, device_id=to, device_id_type=MESH
        )

    def wait_for(ref, sem):
        pltpu.make_async_copy(ref, ref, sem).wait()

    def across(src_of, dst, send, got, gl):
        to = x * GROUPS + gl
        for d in range(EXPERTS):
            src = src_of(d)
            copy = remote(src, dst, send, got, (z, (x + d) % EXPERTS, to))
            if d:
                copy.start()
            else:
                own = pltpu.make_async_copy(src, dst, got)
                pl.when(to != t)(copy.start)
                pl.when(to == t)(own.start)

    def across_sent(whole, send, gl):
        to = x * GROUPS + gl

        @pl.when(to == t)
        def _():
            wait_for(whole.at[pl.ds(0, EXPERTS - 1)], send)

        @pl.when(to != t)
        def _():
            wait_for(whole.at[pl.ds(0, EXPERTS)], send)

    def on_core(gl):
        return pl.when(t % GROUPS == gl)

    def sort(gathered, sorted_, q):
        for d in range(EXPERTS):
            for place in range(OWN):
                p = (x + d) % EXPERTS * OWN + place
                value = None
                for e in range(WINDOW):
                    part = gathered[q, e // OWN, e % OWN].reshape(-1, 16, BLK) * sel[p, e][None]
                    value = part if value is None else value + part
                sorted_[q, d, place] = value.reshape(gathered.shape[3:])

    def ring_start(buffer, q, send, go_up, go_down):
        ref = buffer.at[q, z]
        remote(ref, ref, send, go_up.at[q], up).start()
        remote(ref, ref, send, go_down.at[q], down).start()

    def ring_forward(buffer, q, send, go_up, go_down, far):
        n = buffer.shape[2] // 2
        for half, source, got, to in ((0, (z + 3) % SECTIONS, go_up, up), (1, (z + 1) % SECTIONS, go_down, down)):
            wait_for(buffer.at[q, source], got.at[q])
            ref = buffer.at[q, source, pl.ds(half * n, n)]
            remote(ref, ref, send, far.at[q], to).start()

    def ring_finish(buffer, q, far):
        wait_for(buffer.at[q, z], far.at[q])

    def share_of(section, q):
        slot, row = share_place(section, q % CHUNKS_B)
        return packed.at[:, q // CHUNKS_B, slot, pl.ds(pl.multiple_of(row, ROWS_B), ROWS_B)]

    def b_begin(q):
        for d in (2, 1, 3):
            to = (z + d) % SECTIONS
            remote(share_of(to, q), z_b.at[q, z], b_send.at[0, q], b_in.at[q], (to, x, t)).start()
        z_b[q, z] = share_of(z, q)[...]

    def b_route(q):
        gl, i = q // CHUNKS_B, q % CHUNKS_B
        wait_for(z_b.at[q, pl.ds(0, SECTIONS - 1)], b_in.at[q])
        sort(z_b, s_b, q)
        across(lambda d: s_b.at[q, d], fin_b.at[i, z, t], b_send.at[1, q], b_got.at[i], gl)

    def b_spread(q):
        gl, i = q // CHUNKS_B, q % CHUNKS_B

        @on_core(gl)
        def _():
            wait_for(fin_b.at[i, z], b_got.at[i])
            ring_start(fin_b, i, b_ring.at[i], b_up, b_down)

    def b_forward(q):
        i = q % CHUNKS_B

        @on_core(q // CHUNKS_B)
        def _():
            ring_forward(fin_b, i, b_ring.at[i], b_up, b_down, b_far)

    def b_finish(q):
        i = q % CHUNKS_B

        @on_core(q // CHUNKS_B)
        def _():
            ring_finish(fin_b, i, b_far)

    def a_begin(q):
        rows = pl.ds(q % CHUNKS_A * ROWS_A, ROWS_A)
        z_a[q, z] = packed[:, q // CHUNKS_A, pl.ds(0, SLOTS_A), rows]
        ring_start(z_a, q, a_send.at[0, q], a_up, a_down)

    def a_forward(q):
        ring_forward(z_a, q, a_send.at[0, q], a_up, a_down, a_far)

    def a_route(q):
        gl, i = q // CHUNKS_A, q % CHUNKS_A
        ring_finish(z_a, q, a_far)
        sort(z_a, s_a, q)
        across(lambda d: s_a.at[q, d], fin_a.at[i, t], a_send.at[1, q], a_got.at[i], gl)

    def a_finish(q):
        i = q % CHUNKS_A

        @on_core(q // CHUNKS_A)
        def _():
            wait_for(fin_a.at[i], a_got.at[i])

    def c_begin(_):
        for d in range(1, SECTIONS):
            remote(z_c.at[z], z_c.at[z], c_send.at[0], c_in, ((z + d) % SECTIONS, x, t)).start()

    def c_route(_):
        wait_for(z_c.at[pl.ds(0, SECTIONS - 1)], c_in)
        for gl in range(GROUPS):
            across(lambda d: z_c, fin_c.at[t], c_send.at[1 + gl], c_got, gl)

    def c_finish(_):
        wait_for(fin_c, c_got)

    def load_served(_):
        stage.start()

    def keep_rest(_):
        for le in range(OWN):
            limit = count[z * OWN + le]

            def row_block(r, _, le=le, limit=limit):
                row = pl.ds(pl.multiple_of(r * BLK, BLK), BLK)
                for column in range(2 * GROUPS):
                    block = r * 2 + column % 2
                    sent = 0
                    for j in range(KEEP):
                        chosen = (kept[le, 0, column // 2, j] == block).astype(jnp.int32)
                        sent = sent + chosen * (j < limit).astype(jnp.int32)
                    sent = sent.astype(jnp.float32)
                    at = (column // 2, column % 2 * ROW_BLOCKS + r)
                    change = upd[le][at].astype(jnp.float32) + rest[le][at]
                    rounded = change.astype(jnp.bfloat16).astype(jnp.float32)
                    res_out[le, row, pl.ds(column * BLK, BLK)] = change - sent * rounded
                return 0

            lax.fori_loop(0, ROW_BLOCKS, row_block, 0)

    work = {
        "b": b_begin, "br": b_route, "bs": b_spread, "bf": b_forward, "be": b_finish,
        "a": a_begin, "af": a_forward, "ar": a_route, "ae": a_finish,
        "c": c_begin, "cr": c_route, "ce": c_finish, "k": keep_rest, "l": load_served,
    }
    for item in SCHEDULE:
        name = item.rstrip("0123456789")
        work[name](int(item[len(name) :] or 0))

    for q in range(GROUPS * CHUNKS_B):
        wait_for(z_b.at[q, pl.ds(0, SECTIONS - 1)], b_send.at[0, q])
        across_sent(s_b.at[q], b_send.at[1, q], q // CHUNKS_B)
    for i in range(CHUNKS_B):
        wait_for(fin_b.at[i, pl.ds(0, 3)], b_ring.at[i])
    for q in range(GROUPS * CHUNKS_A):
        wait_for(z_a.at[q, pl.ds(0, 3)], a_send.at[0, q])
        across_sent(s_a.at[q], a_send.at[1, q], q // CHUNKS_A)
    wait_for(z_c.at[pl.ds(0, SECTIONS - 1)], c_send.at[0])
    for gl in range(GROUPS):
        across_sent(fin_c, c_send.at[1 + gl], gl)
    stage.wait()


def by_rows(array):
    return array.reshape(OWN, ROW_BLOCKS, BLK, array.shape[-1])


def push(update, residual, kept, count, slots, served):
    bf = jnp.bfloat16
    hbm, smem, vmem = pltpu.HBM, pltpu.SMEM, pltpu.VMEM
    ca, cb = CHUNKS_A, CHUNKS_B
    na, nb = GROUPS * ca, GROUPS * cb
    dma = pltpu.SemaphoreType.DMA
    return pl.pallas_call(
        push_kernel,
        out_shape=(
            vmem(residual.shape, jnp.float32),
            vmem(served.shape[1:], bf),
            vmem((ca, TENSORS, OWN, SLOTS_A, ROWS_A, BLK), bf),
            vmem((cb, SECTIONS, TENSORS, OWN, ROWS_B, BLK), bf),
            vmem((TENSORS, SECTIONS, 1, BLK), jnp.int32),
        ),
        in_specs=[pl.BlockSpec(memory_space=m) for m in (hbm, hbm, smem, smem, smem, hbm)],
        out_specs=(pl.BlockSpec(memory_space=vmem),) * 5,
        scratch_shapes=[
            *[vmem((GROUPS, 2 * ROW_BLOCKS, BLK, BLK), bf)] * OWN,
            *[vmem((GROUPS, 2 * ROW_BLOCKS, BLK, BLK), jnp.float32)] * OWN,
            vmem((OWN, GROUPS, KEEP, BLK, BLK), bf),
            vmem((WINDOW, WINDOW, 16, BLK), bf),
            vmem((na, SECTIONS, OWN, SLOTS_A, ROWS_A, BLK), bf),
            vmem((na, EXPERTS, OWN, SLOTS_A, ROWS_A, BLK), bf),
            vmem((nb, SECTIONS, OWN, ROWS_B, BLK), bf),
            vmem((nb, EXPERTS, OWN, ROWS_B, BLK), bf),
            vmem((SECTIONS, 1, BLK), jnp.int32),
            dma((OWN, 4 * GROUPS)),
            dma,
            *[dma((2, na)), dma((na,)), dma((na,)), dma((na,)), dma((ca,))],
            *[dma((2, nb)), dma((cb,)), dma((nb,)), dma((cb,)), dma((cb,)), dma((cb,)), dma((cb,))],
            *[dma((3,)), dma, dma],
        ],
        compiler_params=pltpu.CompilerParams(
            collective_id=0, has_side_effects=True, vmem_limit_bytes=45 << 20
        ),
        name="push",
    )(by_rows(update), by_rows(residual), kept, count, slots, served)


def apply_kernel(
    codes_in, count_in, slots_in, rest, staged_in, fin_a, fin_b, out, rest_out, staged,
    codes, count, slots, sem, rest_sem, small_sem,
):
    del staged_in
    rest_copy = pltpu.make_async_copy(rest, rest_out, rest_sem)
    rest_copy.start()
    small = [
        pltpu.make_async_copy(src, dst, small_sem.at[i])
        for i, (src, dst) in enumerate(((codes_in, codes), (count_in, count), (slots_in, slots)))
    ]
    for copy in small:
        copy.start()
    for copy in small:
        copy.wait()
    _, x, t = own_place()

    def region(place, source):
        rows = ROW_BLOCKS * BLK
        at = pl.ds(pl.multiple_of(source * rows, rows), rows)
        return pltpu.make_async_copy(staged.at[place, at], out.at[0, place, at], sem)

    for place in range(OWN):
        p = x * OWN + place
        e = sum(jnp.where(slots[i] == p, i, 0) for i in range(WINDOW))
        limit = count[e]
        base = (e % OWN) * GROUPS * KEEP + (t % GROUPS) * KEEP

        def row_range(source, _):
            for j in range(KEEP):
                code = codes[source, e // OWN, 0, base + j]

                @pl.when(j < limit)
                def _():
                    row = source * (ROW_BLOCKS * BLK) + (code // 2) * BLK
                    column = pl.ds(pl.multiple_of((code % 2) * BLK, BLK), BLK)

                    def add(first, rows, piece):
                        at = (place, pl.ds(pl.multiple_of(row + first, 16), rows), column)
                        total = staged[at].astype(jnp.float32) + piece.astype(jnp.float32)
                        staged[at] = total.astype(jnp.bfloat16)

                    if j < SLOTS_A:
                        for q in range(CHUNKS_A):
                            add(q * ROWS_A, ROWS_A, fin_a[q, source, place, j])
                    else:
                        for section in range(SECTIONS):
                            for q in range(CHUNKS_B):
                                slot, first = share_place(section, q)
                                if slot == j:
                                    add(first, ROWS_B, fin_b[q, section, source, place])

            region(place, source).start()
            return 0

        lax.fori_loop(0, TENSORS, row_range, 0)

    for place in range(OWN):
        for source in range(TENSORS):
            region(place, source).wait()
    rest_copy.wait()


def apply(codes, count, slots, rest, staged, fin_a, fin_b, served):
    smem, vmem = pltpu.SMEM, pltpu.VMEM
    return pl.pallas_call(
        apply_kernel,
        out_shape=(
            jax.ShapeDtypeStruct(served.shape, served.dtype),
            jax.ShapeDtypeStruct(rest.shape, rest.dtype),
            vmem(staged.shape, staged.dtype),
        ),
        in_specs=[pl.BlockSpec(memory_space=pl.ANY)] * 3 + [pl.BlockSpec(memory_space=vmem)] * 4,
        out_specs=[pl.BlockSpec(memory_space=m) for m in (pltpu.HBM, pltpu.HBM, vmem)],
        scratch_shapes=[
            *[smem(a.shape, a.dtype) for a in (codes, count, slots)],
            *[pltpu.SemaphoreType.DMA] * 2,
            pltpu.SemaphoreType.DMA((3,)),
        ],
        input_output_aliases={4: 2},
        compiler_params=pltpu.CompilerParams(vmem_limit_bytes=32 << 20),
        name="apply",
    )(codes, count, slots, rest, staged, fin_a, fin_b)[:2]


def on_device(update, residual, kept_blocks, kept_count, serving_slot, served_up):
    res_new, staged, fin_a, fin_b, codes = push(
        update, residual, kept_blocks, kept_count, serving_slot, served_up
    )
    return apply(codes, kept_count, serving_slot, res_new, staged, fin_a, fin_b, served_up)


def solution(mesh):
    return jax.shard_map(
        on_device,
        mesh=mesh,
        in_specs=(
            P("section", "tensor", "expert"),
            P("section", "tensor", "expert"),
            P("section", "tensor", "expert", None),
            P(),
            P(),
            P("section", "expert", None, "tensor"),
        ),
        out_specs=(P("section", "expert", None, "tensor"), P("section", "tensor", "expert")),
        check_vma=False,
    )
```

```python
import functools

import jax
import jax.numpy as jnp
from jax import lax
from jax.experimental import pallas as pl
from jax.experimental.pallas import tpu as pltpu
from jax.sharding import PartitionSpec as P

MESH = pl.DeviceIdType.MESH
BLK = 128
SECTIONS = 4
EXPERTS = 4
TENSORS = 8
OWN = 2
GROUPS = 2
KEEP = 4
ROW_BLOCKS = 7
WINDOW = 8
SLOTS_A = 1
CHUNKS_A = 1
CHUNKS_B = 3
ROWS_A = BLK // CHUNKS_A
SHARE_B = (KEEP - SLOTS_A) * BLK // SECTIONS
ROWS_B = SHARE_B // CHUNKS_B


SCHEDULE = (
    "c", "b0", "b3", "b1", "b4", "b2", "b5", "a0", "a1", "l", "br0", "br3",
    "br1", "br4", "br2", "br5", "cr", "k", "af0", "bs0", "bs3", "af1", "bs1", "bs4",
    "ar0", "bs2", "bs5", "bf0", "bf3", "ar1", "bf1", "bf4", "bf2", "bf5", "be0", "be3",
    "be1", "be4", "be2", "be5", "ae0", "ae1", "ce",
)


def own_place():
    return lax.axis_index("section"), lax.axis_index("expert"), lax.axis_index("tensor")


def share_place(section, chunk):
    first = section * SHARE_B + chunk * ROWS_B
    return SLOTS_A + first // BLK, first % BLK


def push_kernel(
    update, residual, kept_in, count_in, slots_in, served,
    res_out, staged, fin_a, fin_b, fin_c,
    upd_0, upd_1, rest_0, rest_1, packed, sel, z_a, s_a, z_b, s_b, z_c,
    load_sem, stage_sem, a_send, a_up, a_down, a_far, a_got, b_send, b_ring, b_in, b_got, b_up, b_down, b_far,
    c_send, c_in, c_got, kept, count, slots, small_sem,
):
    z, x, t = own_place()
    up, down = ((z + 1) % SECTIONS, x, t), ((z + 3) % SECTIONS, x, t)
    on_diagonal = t // GROUPS == x

    barrier = pltpu.get_barrier_semaphore()
    for d in range(1, SECTIONS):
        pl.semaphore_signal(barrier, inc=1, device_id=((z + d) % SECTIONS, x, t), device_id_type=MESH)
    for d in range(TENSORS):
        to = (t + d) % TENSORS

        def greet(to=to):
            pl.semaphore_signal(barrier, inc=1, device_id=(z, t // GROUPS, to), device_id_type=MESH)

        if d == 0:
            pl.when(jnp.logical_not(on_diagonal))(greet)
        else:
            greet()

    small = [
        pltpu.make_async_copy(src, dst, small_sem.at[i])
        for i, (src, dst) in enumerate(((kept_in, kept), (count_in, count), (slots_in, slots)))
    ]
    for copy in small:
        copy.start()
    upd, rest = (upd_0, upd_1), (rest_0, rest_1)
    loads = [[] for _ in range(OWN)]
    for le in range(OWN):
        for column in range(2 * GROUPS):
            lanes = pl.ds(column * BLK, BLK)
            for n, (src, dst) in enumerate(((update, upd[le]), (residual, rest[le]))):
                dst = dst.at[column // 2, pl.ds(column % 2 * ROW_BLOCKS, ROW_BLOCKS)]
                loads[le].append(
                    pltpu.make_async_copy(src.at[le, :, :, lanes], dst, load_sem.at[le, 2 * column + n])
                )
    stage = pltpu.make_async_copy(served.at[0], staged, stage_sem)
    for load in (*loads[0], *loads[1]):
        load.start()

    for copy in small:
        copy.wait()
    for p in range(WINDOW):
        for e in range(WINDOW):
            here = (slots[e] == p).astype(jnp.float32)
            sel[p, e] = jnp.full(sel.shape[2:], here, jnp.float32).astype(sel.dtype)
    lanes = lax.broadcasted_iota(jnp.int32, (1, BLK), 1)
    numbers = jnp.zeros((1, BLK), jnp.int32)
    for i in range(OWN * GROUPS * KEEP):
        number = kept[i // (GROUPS * KEEP), 0, i // KEEP % GROUPS, i % KEEP]
        numbers = numbers + number * (lanes == i).astype(jnp.int32)
    z_c[z] = numbers

    for le in range(OWN):
        for load in loads[le]:
            load.wait()
        for gl in range(GROUPS):
            for j in range(KEEP):
                number = kept[le, 0, gl, j]
                at = (gl, (number & 1) * ROW_BLOCKS + (number >> 1))
                change = upd[le][at].astype(jnp.float32) + rest[le][at]
                packed[le, gl, j] = change.astype(jnp.bfloat16)
    pl.semaphore_wait(barrier, SECTIONS - 1 + TENSORS - on_diagonal.astype(jnp.int32))

    def remote(src, dst, send, recv, to):
        return pltpu.make_async_remote_copy(
            src_ref=src, dst_ref=dst, send_sem=send, recv_sem=recv, device_id=to, device_id_type=MESH
        )

    def wait_for(ref, sem):
        pltpu.make_async_copy(ref, ref, sem).wait()

    def across(src_of, dst, send, got, gl):
        to = x * GROUPS + gl
        for d in range(EXPERTS):
            src = src_of(d)
            copy = remote(src, dst, send, got, (z, (x + d) % EXPERTS, to))
            if d:
                copy.start()
            else:
                own = pltpu.make_async_copy(src, dst, got)
                pl.when(to != t)(copy.start)
                pl.when(to == t)(own.start)

    def across_sent(whole, send, gl):
        to = x * GROUPS + gl

        @pl.when(to == t)
        def _():
            wait_for(whole.at[pl.ds(0, EXPERTS - 1)], send)

        @pl.when(to != t)
        def _():
            wait_for(whole.at[pl.ds(0, EXPERTS)], send)

    def on_core(gl):
        return pl.when(t % GROUPS == gl)

    def sort(gathered, sorted_, q):
        for d in range(EXPERTS):
            for place in range(OWN):
                p = (x + d) % EXPERTS * OWN + place
                value = None
                for e in range(WINDOW):
                    part = gathered[q, e // OWN, e % OWN].reshape(-1, 16, BLK) * sel[p, e][None]
                    value = part if value is None else value + part
                sorted_[q, d, place] = value.reshape(gathered.shape[3:])

    def ring_start(buffer, q, send, go_up, go_down):
        ref = buffer.at[q, z]
        remote(ref, ref, send, go_up.at[q], up).start()
        remote(ref, ref, send, go_down.at[q], down).start()

    def ring_forward(buffer, q, send, go_up, go_down, far):
        n = buffer.shape[2] // 2
        for half, source, got, to in ((0, (z + 3) % SECTIONS, go_up, up), (1, (z + 1) % SECTIONS, go_down, down)):
            wait_for(buffer.at[q, source], got.at[q])
            ref = buffer.at[q, source, pl.ds(half * n, n)]
            remote(ref, ref, send, far.at[q], to).start()

    def ring_finish(buffer, q, far):
        wait_for(buffer.at[q, z], far.at[q])

    def share_of(section, q):
        slot, row = share_place(section, q % CHUNKS_B)
        return packed.at[:, q // CHUNKS_B, slot, pl.ds(pl.multiple_of(row, ROWS_B), ROWS_B)]

    def b_begin(q):
        for d in (2, 1, 3):
            to = (z + d) % SECTIONS
            remote(share_of(to, q), z_b.at[q, z], b_send.at[0, q], b_in.at[q], (to, x, t)).start()
        z_b[q, z] = share_of(z, q)[...]

    def b_route(q):
        gl, i = q // CHUNKS_B, q % CHUNKS_B
        wait_for(z_b.at[q, pl.ds(0, SECTIONS - 1)], b_in.at[q])
        sort(z_b, s_b, q)
        across(lambda d: s_b.at[q, d], fin_b.at[i, z, t], b_send.at[1, q], b_got.at[i], gl)

    def b_spread(q):
        gl, i = q // CHUNKS_B, q % CHUNKS_B

        @on_core(gl)
        def _():
            wait_for(fin_b.at[i, z], b_got.at[i])
            ring_start(fin_b, i, b_ring.at[i], b_up, b_down)

    def b_forward(q):
        i = q % CHUNKS_B

        @on_core(q // CHUNKS_B)
        def _():
            ring_forward(fin_b, i, b_ring.at[i], b_up, b_down, b_far)

    def b_finish(q):
        i = q % CHUNKS_B

        @on_core(q // CHUNKS_B)
        def _():
            ring_finish(fin_b, i, b_far)

    def a_begin(q):
        rows = pl.ds(q % CHUNKS_A * ROWS_A, ROWS_A)
        z_a[q, z] = packed[:, q // CHUNKS_A, pl.ds(0, SLOTS_A), rows]
        ring_start(z_a, q, a_send.at[0, q], a_up, a_down)

    def a_forward(q):
        ring_forward(z_a, q, a_send.at[0, q], a_up, a_down, a_far)

    def a_route(q):
        gl, i = q // CHUNKS_A, q % CHUNKS_A
        ring_finish(z_a, q, a_far)
        sort(z_a, s_a, q)
        across(lambda d: s_a.at[q, d], fin_a.at[i, t], a_send.at[1, q], a_got.at[i], gl)

    def a_finish(q):
        i = q % CHUNKS_A

        @on_core(q // CHUNKS_A)
        def _():
            wait_for(fin_a.at[i], a_got.at[i])

    def c_begin(_):
        for d in range(1, SECTIONS):
            remote(z_c.at[z], z_c.at[z], c_send.at[0], c_in, ((z + d) % SECTIONS, x, t)).start()

    def c_route(_):
        wait_for(z_c.at[pl.ds(0, SECTIONS - 1)], c_in)
        for gl in range(GROUPS):
            across(lambda d: z_c, fin_c.at[t], c_send.at[1 + gl], c_got, gl)

    def c_finish(_):
        wait_for(fin_c, c_got)

    def load_served(_):
        stage.start()

    def keep_rest(_):
        for le in range(OWN):
            limit = count[z * OWN + le]

            def row_block(r, _, le=le, limit=limit):
                row = pl.ds(pl.multiple_of(r * BLK, BLK), BLK)
                for column in range(2 * GROUPS):
                    block = r * 2 + column % 2
                    sent = 0
                    for j in range(KEEP):
                        chosen = (kept[le, 0, column // 2, j] == block).astype(jnp.int32)
                        sent = sent + chosen * (j < limit).astype(jnp.int32)
                    sent = sent.astype(jnp.float32)
                    at = (column // 2, column % 2 * ROW_BLOCKS + r)
                    change = upd[le][at].astype(jnp.float32) + rest[le][at]
                    rounded = change.astype(jnp.bfloat16).astype(jnp.float32)
                    res_out[le, row, pl.ds(column * BLK, BLK)] = change - sent * rounded
                return 0

            lax.fori_loop(0, ROW_BLOCKS, row_block, 0)

    work = {
        "b": b_begin, "br": b_route, "bs": b_spread, "bf": b_forward, "be": b_finish,
        "a": a_begin, "af": a_forward, "ar": a_route, "ae": a_finish,
        "c": c_begin, "cr": c_route, "ce": c_finish, "k": keep_rest, "l": load_served,
    }
    for item in SCHEDULE:
        name = item.rstrip("0123456789")
        work[name](int(item[len(name) :] or 0))

    for q in range(GROUPS * CHUNKS_B):
        wait_for(z_b.at[q, pl.ds(0, SECTIONS - 1)], b_send.at[0, q])
        across_sent(s_b.at[q], b_send.at[1, q], q // CHUNKS_B)
    for i in range(CHUNKS_B):
        wait_for(fin_b.at[i, pl.ds(0, 3)], b_ring.at[i])
    for q in range(GROUPS * CHUNKS_A):
        wait_for(z_a.at[q, pl.ds(0, 3)], a_send.at[0, q])
        across_sent(s_a.at[q], a_send.at[1, q], q // CHUNKS_A)
    wait_for(z_c.at[pl.ds(0, SECTIONS - 1)], c_send.at[0])
    for gl in range(GROUPS):
        across_sent(fin_c, c_send.at[1 + gl], gl)
    stage.wait()


def by_rows(array):
    return array.reshape(OWN, ROW_BLOCKS, BLK, array.shape[-1])


def push(update, residual, kept, count, slots, served):
    bf = jnp.bfloat16
    hbm, smem, vmem = pltpu.HBM, pltpu.SMEM, pltpu.VMEM
    ca, cb = CHUNKS_A, CHUNKS_B
    na, nb = GROUPS * ca, GROUPS * cb
    dma = pltpu.SemaphoreType.DMA
    return pl.pallas_call(
        push_kernel,
        out_shape=(
            vmem(residual.shape, jnp.float32),
            vmem(served.shape[1:], bf),
            vmem((ca, TENSORS, OWN, SLOTS_A, ROWS_A, BLK), bf),
            vmem((cb, SECTIONS, TENSORS, OWN, ROWS_B, BLK), bf),
            vmem((TENSORS, SECTIONS, 1, BLK), jnp.int32),
        ),
        in_specs=[pl.BlockSpec(memory_space=m) for m in (hbm, hbm, pl.ANY, pl.ANY, pl.ANY, hbm)],
        out_specs=(pl.BlockSpec(memory_space=vmem),) * 5,
        scratch_shapes=[
            *[vmem((GROUPS, 2 * ROW_BLOCKS, BLK, BLK), bf)] * OWN,
            *[vmem((GROUPS, 2 * ROW_BLOCKS, BLK, BLK), jnp.float32)] * OWN,
            vmem((OWN, GROUPS, KEEP, BLK, BLK), bf),
            vmem((WINDOW, WINDOW, 16, BLK), bf),
            vmem((na, SECTIONS, OWN, SLOTS_A, ROWS_A, BLK), bf),
            vmem((na, EXPERTS, OWN, SLOTS_A, ROWS_A, BLK), bf),
            vmem((nb, SECTIONS, OWN, ROWS_B, BLK), bf),
            vmem((nb, EXPERTS, OWN, ROWS_B, BLK), bf),
            vmem((SECTIONS, 1, BLK), jnp.int32),
            dma((OWN, 4 * GROUPS)),
            dma,
            *[dma((2, na)), dma((na,)), dma((na,)), dma((na,)), dma((ca,))],
            *[dma((2, nb)), dma((cb,)), dma((nb,)), dma((cb,)), dma((cb,)), dma((cb,)), dma((cb,))],
            *[dma((3,)), dma, dma],
            *[smem(a.shape, a.dtype) for a in (kept, count, slots)],
            dma((3,)),
        ],
        compiler_params=pltpu.CompilerParams(
            collective_id=0, has_side_effects=True, vmem_limit_bytes=45 << 20
        ),
        name="push",
    )(by_rows(update), by_rows(residual), kept, count, slots, served)


def apply_kernel(
    codes_in, count_in, slots_in, rest, staged_in, fin_a, fin_b, out, rest_out, staged,
    codes, count, slots, sem, rest_sem, small_sem,
):
    del staged_in
    rest_copy = pltpu.make_async_copy(rest, rest_out, rest_sem)
    rest_copy.start()
    small = [
        pltpu.make_async_copy(src, dst, small_sem.at[i])
        for i, (src, dst) in enumerate(((codes_in, codes), (count_in, count), (slots_in, slots)))
    ]
    for copy in small:
        copy.start()
    for copy in small:
        copy.wait()
    _, x, t = own_place()

    def region(place, source):
        rows = ROW_BLOCKS * BLK
        at = pl.ds(pl.multiple_of(source * rows, rows), rows)
        return pltpu.make_async_copy(staged.at[place, at], out.at[0, place, at], sem)

    for place in range(OWN):
        p = x * OWN + place
        e = sum(jnp.where(slots[i] == p, i, 0) for i in range(WINDOW))
        limit = count[e]
        base = (e % OWN) * GROUPS * KEEP + (t % GROUPS) * KEEP

        def row_range(source, _):
            for j in range(KEEP):
                code = codes[source, e // OWN, 0, base + j]

                @pl.when(j < limit)
                def _():
                    row = source * (ROW_BLOCKS * BLK) + (code // 2) * BLK
                    column = pl.ds(pl.multiple_of((code % 2) * BLK, BLK), BLK)

                    def add(first, rows, piece):
                        at = (place, pl.ds(pl.multiple_of(row + first, 16), rows), column)
                        total = staged[at].astype(jnp.float32) + piece.astype(jnp.float32)
                        staged[at] = total.astype(jnp.bfloat16)

                    if j < SLOTS_A:
                        for q in range(CHUNKS_A):
                            add(q * ROWS_A, ROWS_A, fin_a[q, source, place, j])
                    else:
                        for section in range(SECTIONS):
                            for q in range(CHUNKS_B):
                                slot, first = share_place(section, q)
                                if slot == j:
                                    add(first, ROWS_B, fin_b[q, section, source, place])

            region(place, source).start()
            return 0

        lax.fori_loop(0, TENSORS, row_range, 0)

    for place in range(OWN):
        for source in range(TENSORS):
            region(place, source).wait()
    rest_copy.wait()


def apply(codes, count, slots, rest, staged, fin_a, fin_b, served):
    smem, vmem = pltpu.SMEM, pltpu.VMEM
    return pl.pallas_call(
        apply_kernel,
        out_shape=(
            jax.ShapeDtypeStruct(served.shape, served.dtype),
            jax.ShapeDtypeStruct(rest.shape, rest.dtype),
            vmem(staged.shape, staged.dtype),
        ),
        in_specs=[pl.BlockSpec(memory_space=pl.ANY)] * 3 + [pl.BlockSpec(memory_space=vmem)] * 4,
        out_specs=[pl.BlockSpec(memory_space=m) for m in (pltpu.HBM, pltpu.HBM, vmem)],
        scratch_shapes=[
            *[smem(a.shape, a.dtype) for a in (codes, count, slots)],
            *[pltpu.SemaphoreType.DMA] * 2,
            pltpu.SemaphoreType.DMA((3,)),
        ],
        input_output_aliases={4: 2},
        compiler_params=pltpu.CompilerParams(vmem_limit_bytes=32 << 20),
        name="apply",
    )(codes, count, slots, rest, staged, fin_a, fin_b)[:2]


def on_device(update, residual, kept_blocks, kept_count, serving_slot, served_up):
    res_new, staged, fin_a, fin_b, codes = push(
        update, residual, kept_blocks, kept_count, serving_slot, served_up
    )
    return apply(codes, kept_count, serving_slot, res_new, staged, fin_a, fin_b, served_up)


def solution(mesh):
    return jax.shard_map(
        on_device,
        mesh=mesh,
        in_specs=(
            P("section", "tensor", "expert"),
            P("section", "tensor", "expert"),
            P("section", "tensor", "expert", None),
            P(),
            P(),
            P("section", "expert", None, "tensor"),
        ),
        out_specs=(P("section", "expert", None, "tensor"), P("section", "tensor", "expert")),
        check_vma=False,
    )
```
